256 devices in a mesh: row: 16 (over z_hi, y, core), col: 16 (over x, z_lo).
Axes of the slice: x: 4, y: 4, z: 8 (z_hi: 2, z_lo: 4; z = z_hi * 4 + z_lo), core: 2. Of those that a mesh axis runs over, the one named last changes fastest.
Arguments:
- x_blocks: bfloat16 [16, 16, 8, 128, 128], P('row', 'col'), may hold values from -1.5 to 1.5
- x_rows: int32 [16, 16, 8], replicated, may hold values from 0 to 31, as said below
- x_cols: int32 [16, 16, 8], replicated, may hold values from 0 to 31
- y_rows: int32 [16, 16, 16], replicated, may hold values from 0 to 31, as said below
- y_cols: int32 [16, 16, 16], replicated, may hold values from 0 to 31
- z_rows: int32 [16, 16, 24], replicated, may hold values from 0 to 31, as said below
- z_cols: int32 [16, 16, 24], replicated, may hold values from 0 to 31
Outputs:
- y_blocks: bfloat16 [16, 16, 16, 128, 128], P('row', 'col')
- next_blocks: bfloat16 [16, 16, 24, 128, 128], P('row', 'col')
The draws below stay inside these ranges and needn't reach their ends.
Inputs may be any that keep to these rules, and one draw needn't show every extreme that they name: `x_rows`: together with x_cols: each tile lists exactly 8 distinct block positions, and a block row that appears in a tile appears there exactly 2 times. `y_rows`: together with y_cols: each tile lists exactly 16 distinct block positions. `z_rows`: together with z_cols: each tile lists exactly 24 distinct block positions.
All inputs are finite; a program needn't handle non-finite values.
Results may differ from the reference program's by a relative error of at most 0.0049.
Values may be sent and summed in bfloat16 or wider, within the bound.
No kernel may reach another device: no remote copies, remote signals or barrier semaphores. Data moves between devices by JAX's collectives and lax.ppermute only.
A program may use at most 64 MiB of HBM per device.

```python
import jax
import jax.numpy as jnp
from jax import lax

BLOCK = 128
NBLOCKS = 512
ROW_MOST = 2
X_MOST = 8
SLAB_ROWS = 32
SLAB_COLS = 32
Y_MOST = 16
Z_MOST = 24
N_ROW = 16
N_COL = 16


def tile_pattern(key):
    key = jax.random.fold_in(key, 11)
    key_rows, key_cols = jax.random.split(key, 2)
    tiles = N_ROW * N_COL
    used = X_MOST // ROW_MOST
    rows = jax.vmap(lambda sub: jax.random.permutation(sub, SLAB_ROWS))(jax.random.split(key_rows, tiles))[:, :used]
    cols = jax.vmap(lambda sub: jax.random.permutation(sub, SLAB_COLS))(jax.random.split(key_cols, tiles * used))[:, :ROW_MOST]
    rows_full = jnp.broadcast_to(rows[:, :, None], (tiles, used, ROW_MOST))
    rows_full = rows_full.reshape(N_ROW, N_COL, X_MOST).astype(jnp.int32)
    cols_full = cols.reshape(N_ROW, N_COL, X_MOST).astype(jnp.int32)
    return (rows_full, cols_full)


def dense_from_lists(rows, cols):
    global_rows = (jnp.arange(N_ROW)[:, None, None] * SLAB_ROWS + rows).reshape(-1)
    global_cols = (jnp.arange(N_COL)[None, :, None] * SLAB_COLS + cols).reshape(-1)
    return jnp.zeros((NBLOCKS, NBLOCKS), jnp.int32).at[global_rows, global_cols].set(1)


def choose_positions(key, favour, most):
    tiles = N_ROW * N_COL
    span = SLAB_ROWS * SLAB_COLS
    tiled = favour.reshape(N_ROW, SLAB_ROWS, N_COL, SLAB_COLS).transpose(0, 2, 1, 3).reshape(tiles, span)
    ranks = jax.vmap(lambda sub: jax.random.permutation(sub, span))(jax.random.split(key, tiles))
    scores = tiled * span + ranks
    picked = lax.top_k(scores, most)[1]
    rows = (picked // SLAB_COLS).reshape(N_ROW, N_COL, most).astype(jnp.int32)
    cols = (picked % SLAB_COLS).reshape(N_ROW, N_COL, most).astype(jnp.int32)
    return (rows, cols)


def pattern_product(key):
    rows, cols = tile_pattern(key)
    dense_x = dense_from_lists(rows, cols)
    symbolic = (jnp.dot(dense_x, dense_x) > 0).astype(jnp.int32)
    return choose_positions(jax.random.fold_in(key, 12), symbolic, Y_MOST)


def pattern_result(key):
    rows, cols = tile_pattern(key)
    dense_x = dense_from_lists(rows, cols)
    y_rows, y_cols = pattern_product(key)
    dense_y = dense_from_lists(y_rows, y_cols)
    symbolic = (jnp.dot(dense_x, dense_y) > 0).astype(jnp.int32)
    return choose_positions(jax.random.fold_in(key, 13), symbolic + dense_x, Z_MOST)


def draw_x_rows(key, part):
    return tile_pattern(key)[0]


def draw_x_cols(key, part):
    return tile_pattern(key)[1]


def draw_y_rows(key, part):
    return pattern_product(key)[0]


def draw_y_cols(key, part):
    return pattern_product(key)[1]


def draw_z_rows(key, part):
    return pattern_result(key)[0]


def draw_z_cols(key, part):
    return pattern_result(key)[1]


def steps_of(stream_key, shape, cuts, least, largest):
    loudness, own = 1.0, jax.random.fold_in(stream_key, 6)
    for axis_at, parts in cuts:
        steps = jnp.exp(jax.random.uniform(jax.random.fold_in(own, axis_at), (parts,), jnp.float32, least / len(cuts), largest / len(cuts)))
        loudness = loudness * jnp.repeat(steps, shape[axis_at] // parts).reshape([-1 if axis == axis_at else 1 for axis in range(len(shape))])
    return loudness


def centred(key, dims, spread, limit, shards=(), held_as=jnp.bfloat16):
    entries = spread * jax.random.normal(key, dims, jnp.float32)
    if shards:
        entries = entries * steps_of(key, dims, shards, -0.22, 0.18)
    return jnp.clip(entries, -limit, limit).astype(held_as)


def setup_inputs(seed: int = 0) -> dict:
    streams_of = jax.random.split(jax.random.key(seed), 8)
    return {
        "x_blocks": centred(streams_of[0], (N_ROW, N_COL, X_MOST, BLOCK, BLOCK), (BLOCK // 8) ** -0.5, 1.5, ((0, 16), (1, 16))),
        "x_rows": draw_x_rows(jax.random.fold_in(streams_of[7], 71), 0),
        "x_cols": draw_x_cols(jax.random.fold_in(streams_of[7], 71), 0),
        "y_rows": draw_y_rows(jax.random.fold_in(streams_of[7], 71), 0),
        "y_cols": draw_y_cols(jax.random.fold_in(streams_of[7], 71), 0),
        "z_rows": draw_z_rows(jax.random.fold_in(streams_of[7], 71), 0),
        "z_cols": draw_z_cols(jax.random.fold_in(streams_of[7], 71), 0),
    }


def contract(left, left_index, left_mask, right, right_index, right_mask):
    shape = left_index.shape[:3]
    inner_count = N_COL * ROW_MOST

    def single(items):
        left_at, left_ok, right_at, right_ok = items
        left_part = jnp.where(left_ok[:, :, None, None], left[left_at], 0.0).astype(jnp.float32)
        right_part = jnp.where(right_ok[:, :, None, None], right[right_at], 0.0).astype(jnp.float32)
        return jnp.einsum("nqab,nqbc->nac", left_part, right_part, precision=lax.Precision.HIGHEST)

    count = left_index.size // inner_count
    group = 16
    padded = (count + group - 1) // group * group

    def prepare(values):
        flat = values.reshape(count, inner_count)
        flat = jnp.concatenate([flat, jnp.zeros((padded - count, inner_count), flat.dtype)], axis=0)
        return flat.reshape(padded // group, group, inner_count)

    result = lax.map(single, (prepare(left_index), prepare(left_mask), prepare(right_index), prepare(right_mask)))
    result = result.reshape(padded, BLOCK, BLOCK)[:count]
    return result.reshape(shape + (BLOCK, BLOCK))


def left_plan(x_rows, x_cols, out_local, tile_row):
    left_rows = x_rows[tile_row]
    left_cols = x_cols[tile_row]
    hit = left_rows == out_local[..., None, None]
    rank = jnp.cumsum(hit.astype(jnp.int32), axis=-1) - 1
    picks = hit[..., None, :] & (rank[..., None, :] == jnp.arange(ROW_MOST).astype(jnp.int32)[:, None])
    weights = picks.astype(jnp.int32)
    left_mask = jnp.any(picks, axis=-1)
    slot = jnp.sum(weights * jnp.arange(X_MOST).astype(jnp.int32), axis=-1).astype(jnp.int32)
    columns = jnp.sum(weights * left_cols[..., None, :], axis=-1).astype(jnp.int32)
    sections = jnp.arange(N_COL).astype(jnp.int32)[:, None]
    inner = (sections * SLAB_COLS + columns).astype(jnp.int32)
    left_index = (tile_row[..., None, None] * N_COL + sections) * X_MOST + slot
    left_index = jnp.where(left_mask, left_index, 0).astype(jnp.int32)
    return left_mask, left_index, inner


def right_plan(table_rows, table_cols, inner, left_mask, out_cols, tile_col, most):
    owner = (inner // SLAB_ROWS).astype(jnp.int32)
    within = (inner % SLAB_ROWS).astype(jnp.int32)
    column_here = jnp.broadcast_to(tile_col[..., None, None], inner.shape).astype(jnp.int32)
    matched = (table_rows[owner, column_here] == within[..., None]) & (table_cols[owner, column_here] == out_cols[..., None, None, None])
    found = left_mask & jnp.any(matched, axis=-1)
    slot = jnp.sum(matched.astype(jnp.int32) * jnp.arange(most).astype(jnp.int32), axis=-1).astype(jnp.int32)
    index = jnp.where(found, (owner * N_COL + column_here) * most + slot, 0).astype(jnp.int32)
    return found, index


def reference(x_blocks, x_rows, x_cols, y_rows, y_cols, z_rows, z_cols):
    flat_x = x_blocks.reshape(-1, BLOCK, BLOCK)
    tile_row = jnp.broadcast_to(jnp.arange(N_ROW).astype(jnp.int32)[:, None, None], y_rows.shape)
    tile_col = jnp.broadcast_to(jnp.arange(N_COL).astype(jnp.int32)[None, :, None], y_rows.shape)
    left_mask, left_index, inner = left_plan(x_rows, x_cols, y_rows, tile_row)
    right_mask, right_index = right_plan(x_rows, x_cols, inner, left_mask, y_cols, tile_col, X_MOST)
    y_blocks = contract(flat_x, left_index, left_mask, flat_x, right_index, right_mask).astype(jnp.bfloat16)

    flat_y = y_blocks.reshape(-1, BLOCK, BLOCK)
    tile_row_z = jnp.broadcast_to(jnp.arange(N_ROW).astype(jnp.int32)[:, None, None], z_rows.shape)
    tile_col_z = jnp.broadcast_to(jnp.arange(N_COL).astype(jnp.int32)[None, :, None], z_rows.shape)
    left_mask_z, left_index_z, inner_z = left_plan(x_rows, x_cols, z_rows, tile_row_z)
    found, right_index_z = right_plan(y_rows, y_cols, inner_z, left_mask_z, z_cols, tile_col_z, Y_MOST)
    z_total = contract(flat_x, left_index_z, left_mask_z, flat_y, right_index_z, found)

    here = (x_rows[tile_row_z, tile_col_z] == z_rows[..., None]) & (x_cols[tile_row_z, tile_col_z] == z_cols[..., None])
    present = jnp.any(here, axis=-1)
    own_slot = jnp.sum(here.astype(jnp.int32) * jnp.arange(X_MOST).astype(jnp.int32), axis=-1)
    own_index = jnp.where(present, (tile_row_z * N_COL + tile_col_z) * X_MOST + own_slot, 0).astype(jnp.int32)
    x_here = jnp.where(present[..., None, None], flat_x[own_index], 0.0).astype(jnp.float32)
    next_blocks = (1.5 * x_here - 0.5 * z_total).astype(jnp.bfloat16)
    return y_blocks, next_blocks
```

```python
import functools

import jax
import jax.numpy as jnp
from jax import lax
from jax.experimental import pallas as pl
from jax.experimental.pallas import tpu as pltpu
from jax.sharding import PartitionSpec as P

SLAB = 32
SIDE = 16
BLOCK = 128
TERMS = 32
COUNT = 32
OWN = 33
FLAG = 34
LEFT_FIRST = 10
LEFT_ALL = 17
RIGHT_FIRST = 10
MOST = 32

ROW = [(z, y, k) for z in range(2) for y in range(4) for k in range(2)]
COL = [(x, b) for x in range(4) for b in range(4)]


def row_at(z, y, k):
    return z * 8 + y % 4 * 2 + k


def col_at(x, b):
    return x % 4 * 4 + b


Z_SWAP = [(row_at(z, y, k), row_at(1 - z, y, k)) for z, y, k in ROW]
CORE_SWAP = [(row_at(z, y, k), row_at(z, y, 1 - k)) for z, y, k in ROW]
Y_RING = [[(row_at(z, y, k), row_at(z, y + d, k)) for z, y, k in ROW] for d in (1, 3, 2)]
X_RING = [[(col_at(x, b), col_at(x + d, b)) for x, b in COL] for d in (1, 3, 2)]
B_SWAP = [[(col_at(x, b), col_at(x, b ^ d)) for x, b in COL] for d in (1, 2, 3)]


def ring_piece(offset):
    return jnp.where(offset == 0, 0, jnp.where(offset == 1, 2, jnp.where(offset == 2, 3, 1)))


def iota(shape, dim):
    return lax.broadcasted_iota(jnp.int32, shape, dim)


def half(values):
    return values.astype(jnp.float32).astype(jnp.bfloat16)


def nn(a, b):
    return jnp.dot(half(a), half(b), preferred_element_type=jnp.float32)


def nt(a, b):
    return lax.dot_general(
        half(a), half(b), (((1,), (1,)), ((), ())), preferred_element_type=jnp.float32
    )


def eye(size):
    return iota((size, size), 0) == iota((size, size), 1)


def flat(table, by_col):
    most = table.shape[-1]
    size = SIDE * most
    values = table[...].reshape(SIDE * SIDE, most)
    wide = nn(values, (iota((most, size), 1) & (most - 1)) == iota((most, size), 0))
    tile = iota((SIDE * SIDE, size), 0)
    section = iota((SIDE * SIDE, size), 1) // most
    pick = iota((SIDE, SIDE * SIDE), 1)
    if by_col:
        wide = jnp.where(section == tile >> 4, wide, 0.0)
        pick = pick & 15
    else:
        wide = jnp.where(section == tile & 15, wide, 0.0)
        pick = pick >> 4
    return nn(pick == iota((SIDE, SIDE * SIDE), 0), wide)


def slab(table, row):
    most = table.shape[-1]
    size = SIDE * most
    wide = nn(table[row], (iota((most, size), 1) & (most - 1)) == iota((most, size), 0))
    wide = jnp.where(iota((SIDE, size), 1) // most == iota((SIDE, size), 0), wide, 0.0)
    return jnp.sum(wide, axis=0, keepdims=True)


def pick_row(values, index):
    return nn(iota((8, values.shape[0]), 1) == index, values)


def to_col(lanes):
    size = lanes.shape[1]
    return nt(eye(size), jnp.broadcast_to(lanes[:1], (8, size)))[:, :1]


def start_of(size, most, dim):
    shape = (1, size) if dim else (size, 1)
    return ((iota(shape, dim) // most) * SLAB).astype(jnp.float32)


def message(ranks, dest, mine, place):
    size, dests = ranks.shape
    rank = nn(ranks, iota((dests, 8), 0) == dest)[:, :1]
    lane = iota((size, 128), 1)
    slots = (rank == (lane + 1).astype(jnp.float32)) & mine
    return nn(jnp.broadcast_to(place, (8, size)), slots)[:1]


def table_of(rows, flag):
    sub, lane = iota((8, 128), 0), iota((8, 128), 1)
    table = jnp.where((sub == 3) & (lane == 0), flag, 0.0)
    for n, values in enumerate(rows):
        table = jnp.where(sub == n, values, table)
    return table.astype(jnp.int32)


def left_kernel(at, x_rows, x_cols, y_rows, y_cols, z_rows, z_cols, send, positions):
    row, col = at[0], at[1]
    x, b = col >> 2, col & 3
    n = SIDE * x_rows.shape[-1]
    left_i = to_col(slab(x_rows, row))
    left_k = to_col(slab(x_cols, row)) + start_of(n, x_rows.shape[-1], 0)

    def needed(rows, cols, out_rows, out_cols):
        most = rows.shape[-1]
        outs = out_rows.shape[-1]
        keys = flat(rows, True) + start_of(SIDE * most, most, 1)
        others = flat(cols, True)
        out_i = out_rows[row].astype(jnp.float32)
        out_j = nt(eye(outs), out_cols[row])
        result = jnp.zeros((n, SIDE), jnp.float32)
        for c in range(SIDE):
            same_k = left_k == keys[c : c + 1]
            same_j = out_j[:, c : c + 1] == others[c : c + 1]
            hit = (nt(same_k, same_j) > 0.5) & (left_i == out_i[c : c + 1])
            some = jnp.max(hit.astype(jnp.float32), axis=1, keepdims=True)
            result = jnp.where(iota((n, SIDE), 1) == c, some, result)
        return result

    for_y = needed(x_rows, x_cols, y_rows, y_cols)
    for_z = needed(y_rows, y_cols, z_rows, z_cols) * (1.0 - for_y)
    group = iota((n, n), 0) >> 3 & 3
    same = group == (iota((n, n), 1) >> 3 & 3)
    before = same & (iota((n, n), 1) <= iota((n, n), 0))
    total_y, total_z = nn(same, for_y), nn(same, for_z)
    ranks = jnp.where(
        for_y > 0.5, nn(before, for_y), jnp.where(for_z > 0.5, total_y + nn(before, for_z), 0.0)
    )
    crosses = (iota((n, SIDE), 0) >> 3 & 3) != (iota((n, SIDE), 1) & 3)
    over = crosses & ((total_y > LEFT_FIRST) | (total_y + total_z > LEFT_ALL))
    flag = jnp.max(over.astype(jnp.float32))

    lane = iota((1, n), 1)
    place = (ring_piece((lane >> 5) - x & 3) * 8 + (lane & 7)).astype(jnp.float32)
    mine = (iota((n, 1), 0) >> 3 & 3) == b
    rows = [message(ranks, (x << 2) + (b ^ d), mine, place) for d in (1, 2, 3)]
    send[...] = table_of(rows, flag)
    rank = nt(iota((8, SIDE), 1) == col, ranks)[:1]
    d = (lane >> 3 & 3) ^ b
    spot = jnp.where(d == 0, place, (d * MOST).astype(jnp.float32) + jnp.maximum(rank - 1.0, 0.0))
    positions[...] = jnp.broadcast_to(spot, (8, n)).astype(jnp.int32)


def terms_list(out_i, out_j, left_i, left_k, left_pos, right_k, right_j, right_pos):
    outs, size = out_i.shape[0], left_i.shape[1]
    found = nt(jnp.where(out_j == right_j, right_pos + 1.0, 0.0), left_k == right_k)
    hit = (out_i == left_i) & (found > 0.5)
    marks = hit.astype(jnp.float32)
    rank = nn(marks, iota((size, size), 0) <= iota((size, size), 1))
    code = left_pos * 256.0 + (found - 1.0)
    lane = iota((outs, 128), 1)
    table = jnp.where(lane == COUNT, jnp.sum(marks, axis=1, keepdims=True), 0.0)
    for q in range(TERMS):
        picked = jnp.where(hit & (rank == q + 1.0), code, 0.0)
        table = table + jnp.where(lane == q, jnp.sum(picked, axis=1, keepdims=True), 0.0)
    return table, lane


def right_kernel(
    at, left_send, positions, x_rows, x_cols, y_rows, y_cols, z_rows, z_cols, send, y_plan, z_plan
):
    row, col = at[0], at[1]
    z, y, k = row >> 3, row >> 1 & 3, row & 1
    most, y_most, z_most = x_rows.shape[-1], y_rows.shape[-1], z_rows.shape[-1]
    n, m = SIDE * most, SIDE * y_most
    rows_i = flat(x_rows, False)
    rows_k = flat(x_cols, False) + start_of(n, most, 1)
    y_i = pick_row(flat(y_rows, True), col)[:1]
    y_j = pick_row(flat(y_cols, True), col)[:1]
    key = to_col(y_i) + start_of(m, y_most, 0)
    other = to_col(y_j)
    tile = iota((SIDE, SIDE * SIDE), 1)
    ours = (tile >> 4 == iota((SIDE, SIDE * SIDE), 0)) & ((tile & 15) == col)
    z_i = nn(ours, z_rows[...].reshape(SIDE * SIDE, z_most))
    z_j = nn(ours, z_cols[...].reshape(SIDE * SIDE, z_most))
    z_t = nt(eye(z_most), z_i)
    need = jnp.zeros((m, SIDE), jnp.float32)
    for r in range(SIDE):
        same_k = key == rows_k[r : r + 1]
        same_i = z_t[:, r : r + 1] == rows_i[r : r + 1]
        hit = (nt(same_k, same_i) > 0.5) & (other == z_j[r : r + 1])
        some = jnp.max(hit.astype(jnp.float32), axis=1, keepdims=True)
        need = jnp.where(iota((m, SIDE), 1) == r, some, need)
    need = nn(need, iota((SIDE, 8), 0) >> 1 == iota((SIDE, 8), 1)) > 0.5
    same = iota((m, m), 0) >> 4 == iota((m, m), 1) >> 4
    before = same & (iota((m, m), 1) <= iota((m, m), 0))
    ranks = jnp.where(need, nn(before, need), 0.0)
    crosses = (iota((m, 8), 0) >> 5 & 3) != (iota((m, 8), 1) & 3)
    over = crosses & (nn(same, need) > RIGHT_FIRST)
    flag = jnp.max(over.astype(jnp.float32))

    lane = iota((1, m), 1)
    slot = (lane & 15).astype(jnp.float32)
    tile = iota((m, 1), 0) >> 4
    dests = [(z << 2) + (y + d & 3) for d in (1, 3, 2)]
    rows = [message(ranks, dest, tile == row, slot) for dest in dests]
    send[:8] = table_of(rows, flag)
    rows = [message(ranks, dest, tile == (row ^ 8), slot) for dest in dests]
    send[8:] = table_of(rows, flag)
    rank = nt(iota((8, 8), 1) == row >> 1, ranks)[:1]
    piece = ring_piece((lane >> 5 & 3) - y & 3)
    spot = jnp.where(piece == 0, slot, jnp.maximum(rank - 1.0, 0.0))
    base = (lane >> 4 & 1 ^ k) * 128 + piece * MOST + (lane >> 7 ^ z) * 16
    y_pos = base.astype(jnp.float32) + spot
    lane = iota((1, n), 1)
    piece = ring_piece((lane >> 4 & 3) - y & 3)
    x_pos = (lane >> 3 & 1 ^ k) * 64 + piece * 16 + (lane >> 6 ^ z) * 8 + (lane & 7)
    x_pos = x_pos.astype(jnp.float32)

    x_k = pick_row(flat(x_rows, True), col)[:1] + start_of(n, most, 1)
    x_j = pick_row(flat(x_cols, True), col)[:1]
    left_i = slab(x_rows, row)
    left_k = to_col(slab(x_cols, row)) + start_of(n, most, 0)
    left_pos = positions[:1].astype(jnp.float32)

    def own(table):
        return pick_row(table[row], col)[:1]

    left_flag = left_send[3, 0].astype(jnp.float32)
    table, lane = terms_list(
        to_col(own(y_rows)), to_col(own(y_cols)), left_i, left_k, left_pos, x_k, x_j, x_pos
    )
    y_plan[...] = jnp.where(lane == FLAG, left_flag, table).astype(jnp.int32)
    out_i, out_j = to_col(own(z_rows)), to_col(own(z_cols))
    table, lane = terms_list(
        out_i, out_j, left_i, left_k, left_pos,
        y_i + start_of(m, y_most, 1), y_j, y_pos,
    )
    here = (own(x_rows) == out_i) & (own(x_cols) == out_j)
    slot = (iota(here.shape, 1) + 1).astype(jnp.float32)
    slot = jnp.sum(jnp.where(here, slot, 0.0), axis=1, keepdims=True)
    table = table + jnp.where(lane == OWN, slot, 0.0)
    table = jnp.where(lane == FLAG, left_flag + 2.0 * flag, table)
    z_plan[...] = table.astype(jnp.int32)


def pack_kernel(unit, count, first_row, start, sizes, table, *refs):
    sources, outs = refs[:count], refs[count : count + 3 * len(sizes)]
    held, in_sems, out_sems = refs[count + 3 * len(sizes) :]
    loads = [
        pltpu.make_async_copy(source, held.at[pl.ds(n * unit, unit)], in_sems.at[n])
        for n, source in enumerate(sources)
    ]
    for load in loads:
        load.start()
    for load in loads:
        load.wait()
    copies = []
    at = start
    for group, size in enumerate(sizes):
        for n in range(size):
            for d in range(3):
                copies.append(
                    pltpu.make_async_copy(
                        held.at[table[first_row + d, at + n]],
                        outs[group * 3 + d].at[n],
                        out_sems.at[len(copies)],
                    )
                )
        at += size
    for copy in copies:
        copy.start()
    for copy in copies:
        copy.wait()


def pack(table, sources, first_row, start, *sizes):
    unit = sources[0].shape[0]
    return pl.pallas_call(
        functools.partial(pack_kernel, unit, len(sources), first_row, start, sizes),
        out_shape=[
            jax.ShapeDtypeStruct((size, BLOCK, BLOCK), jnp.bfloat16)
            for size in sizes
            for _ in range(3)
        ],
        in_specs=[pl.BlockSpec(memory_space=pltpu.SMEM)]
        + [pl.BlockSpec(memory_space=pl.ANY)] * len(sources),
        out_specs=[pl.BlockSpec(memory_space=pl.ANY)] * (3 * len(sizes)),
        scratch_shapes=[
            pltpu.VMEM((unit * len(sources), BLOCK, BLOCK), jnp.bfloat16),
            pltpu.SemaphoreType.DMA((len(sources),)),
            pltpu.SemaphoreType.DMA((3 * sum(sizes),)),
        ],
    )(table, *sources)


def nothing(count, size):
    return pl.pallas_call(
        lambda *refs: None,
        out_shape=[jax.ShapeDtypeStruct((size, BLOCK, BLOCK), jnp.bfloat16)] * count,
        out_specs=[pl.BlockSpec(memory_space=pl.ANY)] * count,
    )()


def products_kernel(layout, update, plan, *refs):
    pieces = refs[: len(layout)]
    out, left, right, total, sems = refs[len(layout) :]

    def copy(n):
        side, at, skip, size, _ = layout[n]
        buffer = (left, right)[side]
        source = pieces[n] if skip is None else pieces[n].at[pl.ds(skip, size)]
        return pltpu.make_async_copy(source, buffer.at[pl.ds(at, size)], sems.at[n])

    def each(act):
        for n, piece in enumerate(layout):
            if piece[4]:

                @pl.when(plan[0, FLAG] & piece[4] != 0)
                def _():
                    act(copy(n))

            else:
                act(copy(n))

    each(lambda c: c.start())
    each(lambda c: c.wait())

    def product(t, q):
        code = plan[t, q]
        return jnp.dot(
            left[code >> 8], right[code & 255], preferred_element_type=jnp.float32
        )

    outs = out.shape[0]
    for t in range(outs):
        total[t] = jnp.where(plan[t, COUNT] > 0, product(t, 0), 0.0)

    def more(t, carry):
        def term(q, inner):
            total[t] += product(t, q)
            return inner

        return lax.fori_loop(1, plan[t, COUNT], term, carry)

    lax.fori_loop(0, outs, more, 0)
    for t in range(outs):
        if update:
            slot = plan[t, OWN]
            x_here = left[jnp.maximum(slot - 1, 0)].astype(jnp.float32)
            x_here = jnp.where(slot > 0, x_here, 0.0)
            out[t] = (1.5 * x_here - 0.5 * total[t]).astype(jnp.bfloat16)
        else:
            out[t] = total[t].astype(jnp.bfloat16)


def products(plan, pieces, sizes, update):
    outs = plan.shape[0]
    layout = [
        (side, at, skip, p.shape[0] - (skip or 0), bit) for side, at, skip, bit, p in pieces
    ]
    return pl.pallas_call(
        functools.partial(products_kernel, layout, update),
        out_shape=jax.ShapeDtypeStruct((outs, BLOCK, BLOCK), jnp.bfloat16),
        in_specs=[pl.BlockSpec(memory_space=pltpu.SMEM)]
        + [pl.BlockSpec(memory_space=pl.ANY)] * len(pieces),
        out_specs=pl.BlockSpec(memory_space=pltpu.VMEM),
        scratch_shapes=[
            pltpu.VMEM((sizes[0], BLOCK, BLOCK), jnp.bfloat16),
            pltpu.VMEM((sizes[1], BLOCK, BLOCK), jnp.bfloat16),
            pltpu.VMEM((outs, BLOCK, BLOCK), jnp.float32),
            pltpu.SemaphoreType.DMA((len(pieces),)),
        ],
        compiler_params=pltpu.CompilerParams(vmem_limit_bytes=32 * 1024 * 1024),
    )(plan, *[p[-1] for p in pieces])


def row_send(blocks, perm):
    return lax.ppermute(blocks, "row", perm)


def col_send(blocks, perm):
    return lax.ppermute(blocks, "col", perm)


def after(value, *others):
    return lax.optimization_barrier((value, others))[0]


def shards(x_blocks, x_rows, x_cols, y_rows, y_cols, z_rows, z_cols):
    row = lax.axis_index("row")
    col = lax.axis_index("col")
    at = jnp.stack([row, col]).astype(jnp.int32)
    tables = (x_rows, x_cols, y_rows, y_cols, z_rows, z_cols)
    tile = x_blocks[0, 0]
    y_most, z_most = y_rows.shape[-1], z_rows.shape[-1]
    smem = pl.BlockSpec(memory_space=pltpu.SMEM)
    vmem = pl.BlockSpec(memory_space=pltpu.VMEM)

    far = row_send(tile, Z_SWAP)
    near = [col_send(tile, ring) for ring in X_RING]
    left_send, positions = pl.pallas_call(
        left_kernel,
        out_shape=(jax.ShapeDtypeStruct((8, 128), jnp.int32),) * 2,
        in_specs=[smem] + [vmem] * 6,
    )(at, *tables)
    near, left_send, positions = lax.optimization_barrier((near, left_send, positions))
    quad = [tile] + near
    first = pack(left_send, quad, 0, 0, LEFT_FIRST, LEFT_ALL - LEFT_FIRST)
    first, far = lax.optimization_barrier((first, far))
    first, second = first[:3], first[3:]
    first = [col_send(blocks, swap) for blocks, swap in zip(first, B_SWAP)]
    pair = jnp.concatenate([tile, far])
    across = row_send(pair, Y_RING[2])
    up = row_send(pair, Y_RING[0])
    down = row_send(after(pair, first[0]), Y_RING[1])
    pair_mate = row_send(after(pair, first[0]), CORE_SWAP)
    right_send, y_plan, z_plan = pl.pallas_call(
        right_kernel,
        out_shape=(
            jax.ShapeDtypeStruct((16, 128), jnp.int32),
            jax.ShapeDtypeStruct((y_most, 128), jnp.int32),
            jax.ShapeDtypeStruct((z_most, 128), jnp.int32),
        ),
        in_specs=[smem, smem] + [vmem] * 7,
    )(at, left_send, positions, *tables)
    first, up, down, across, pair_mate, right_send, y_plan, z_plan = lax.optimization_barrier(
        (first, up, down, across, pair_mate, right_send, y_plan, z_plan)
    )
    x_half = [pair, up, down, across]
    x_mate = [pair_mate] + [row_send(blocks, CORE_SWAP) for blocks in x_half[1:]]
    one = col_send(second[0], B_SWAP[0])

    def more_left():
        rest = pack(left_send, quad, 0, LEFT_FIRST, MOST - LEFT_FIRST)
        return tuple(col_send(blocks, swap) for blocks, swap in zip(rest, B_SWAP))

    rest = lax.cond(
        left_send[3, 0] > 0, more_left, lambda: tuple(nothing(3, MOST - LEFT_FIRST))
    )

    left = [(0, 8 * n, None, 0, p) for n, p in enumerate(quad)]
    left += [(0, MOST * (n + 1), None, 0, p) for n, p in enumerate(first)]
    right = [(1, 16 * n, None, 0, p) for n, p in enumerate(x_half + x_mate)]
    extra = [(0, MOST * (n + 1) + LEFT_FIRST, None, 1, p) for n, p in enumerate(rest)]
    y_tile = products(y_plan, left + right + extra, (4 * MOST, 128), False)

    y_far = row_send(y_tile, Z_SWAP)
    tile_mate = row_send(y_tile, CORE_SWAP)
    own_send = pack(right_send, [y_tile], 0, 0, RIGHT_FIRST)
    own_near = [row_send(blocks, ring) for blocks, ring in zip(own_send, Y_RING)]
    y_far, tile_mate, own_near, one = lax.optimization_barrier((y_far, tile_mate, own_near, one))
    far_send = pack(right_send, [y_far], 8, 0, RIGHT_FIRST)
    far_mate = row_send(y_far, CORE_SWAP)
    far_send, far_mate = lax.optimization_barrier((far_send, far_mate))
    far_near = [row_send(blocks, ring) for blocks, ring in zip(far_send, Y_RING)]
    second = [one] + [col_send(blocks, swap) for blocks, swap in zip(second[1:], B_SWAP[1:])]
    own_mate = [row_send(blocks, CORE_SWAP) for blocks in own_near]
    far_near, second, own_mate = lax.optimization_barrier((far_near, second, own_mate))
    far_near_mate = [row_send(blocks, CORE_SWAP) for blocks in far_near]

    def more_right():
        blocks = pack(right_send, [y_tile], 0, RIGHT_FIRST, y_most - RIGHT_FIRST)
        blocks += pack(right_send, [y_far], 8, RIGHT_FIRST, y_most - RIGHT_FIRST)
        blocks = [row_send(b, ring) for b, ring in zip(blocks, Y_RING + Y_RING)]
        return tuple(blocks + [row_send(b, CORE_SWAP) for b in blocks])

    more = lax.cond(
        right_send[3, 0] > 0, more_right, lambda: tuple(nothing(12, y_most - RIGHT_FIRST))
    )

    left += [(0, MOST * (n + 1) + LEFT_FIRST, None, 0, p) for n, p in enumerate(second)]
    extra = [
        (0, MOST * (n + 1) + LEFT_ALL, LEFT_ALL - LEFT_FIRST, 1, p) for n, p in enumerate(rest)
    ]
    right = []
    spots = [i * MOST + j * y_most for i in range(4) for j in range(2)]
    ours = [y_tile, y_far] + [p for both in zip(own_near, far_near) for p in both]
    theirs = [tile_mate, far_mate] + [p for both in zip(own_mate, far_near_mate) for p in both]
    for n, side in enumerate((ours, theirs)):
        right += [(1, n * 128 + spot, None, 0, p) for spot, p in zip(spots, side)]
        rest_spots = spots[2::2] + spots[3::2]
        extra += [
            (1, n * 128 + spot + RIGHT_FIRST, None, 2, p)
            for spot, p in zip(rest_spots, more[6 * n : 6 * n + 6])
        ]
    update = products(z_plan, left + right + extra, (4 * MOST, 8 * MOST), True)
    return (y_tile[None, None], update[None, None])


def solution(mesh):
    in_specs = (P("row", "col", None, None, None), P(), P(), P(), P(), P(), P())
    out_specs = (P("row", "col", None, None, None), P("row", "col", None, None, None))
    return jax.shard_map(shards, mesh=mesh, in_specs=in_specs, out_specs=out_specs, check_vma=False)
```

```python
import functools

import jax
import jax.numpy as jnp
from jax import lax
from jax.experimental import pallas as pl
from jax.experimental.pallas import tpu as pltpu
from jax.sharding import PartitionSpec as P

SLAB = 32
SIDE = 16
BLOCK = 128
TERMS = 32
COUNT = 32
OWN = 33
FLAG = 34
MULTIS = 35
MULTI = 40
LEFT_FIRST = 10
LEFT_ALL = 17
RIGHT_FIRST = 10
MOST = 32

ROW = [(z, y, k) for z in range(2) for y in range(4) for k in range(2)]
COL = [(x, b) for x in range(4) for b in range(4)]


def row_at(z, y, k):
    return z * 8 + y % 4 * 2 + k


def col_at(x, b):
    return x % 4 * 4 + b


Z_SWAP = [(row_at(z, y, k), row_at(1 - z, y, k)) for z, y, k in ROW]
CORE_SWAP = [(row_at(z, y, k), row_at(z, y, 1 - k)) for z, y, k in ROW]
Y_RING = [[(row_at(z, y, k), row_at(z, y + d, k)) for z, y, k in ROW] for d in (1, 3, 2)]
X_RING = [[(col_at(x, b), col_at(x + d, b)) for x, b in COL] for d in (1, 3, 2)]
B_SWAP = [[(col_at(x, b), col_at(x, b ^ d)) for x, b in COL] for d in (1, 2, 3)]


def ring_piece(offset):
    return jnp.where(offset == 0, 0, jnp.where(offset == 1, 2, jnp.where(offset == 2, 3, 1)))


def iota(shape, dim):
    return lax.broadcasted_iota(jnp.int32, shape, dim)


def half(values):
    return values.astype(jnp.float32).astype(jnp.bfloat16)


def nn(a, b):
    return jnp.dot(half(a), half(b), preferred_element_type=jnp.float32)


def nt(a, b):
    return lax.dot_general(
        half(a), half(b), (((1,), (1,)), ((), ())), preferred_element_type=jnp.float32
    )


def eye(size):
    return iota((size, size), 0) == iota((size, size), 1)


def flat(table, by_col):
    most = table.shape[-1]
    size = SIDE * most
    values = table[...].reshape(SIDE * SIDE, most)
    wide = nn(values, (iota((most, size), 1) & (most - 1)) == iota((most, size), 0))
    tile = iota((SIDE * SIDE, size), 0)
    section = iota((SIDE * SIDE, size), 1) // most
    pick = iota((SIDE, SIDE * SIDE), 1)
    if by_col:
        wide = jnp.where(section == tile >> 4, wide, 0.0)
        pick = pick & 15
    else:
        wide = jnp.where(section == tile & 15, wide, 0.0)
        pick = pick >> 4
    return nn(pick == iota((SIDE, SIDE * SIDE), 0), wide)


def slab(table, row):
    most = table.shape[-1]
    size = SIDE * most
    wide = nn(table[row], (iota((most, size), 1) & (most - 1)) == iota((most, size), 0))
    wide = jnp.where(iota((SIDE, size), 1) // most == iota((SIDE, size), 0), wide, 0.0)
    return jnp.sum(wide, axis=0, keepdims=True)


def pick_row(values, index):
    return nn(iota((8, values.shape[0]), 1) == index, values)


def to_col(lanes):
    size = lanes.shape[1]
    return nt(eye(size), jnp.broadcast_to(lanes[:1], (8, size)))[:, :1]


def start_of(size, most, dim):
    shape = (1, size) if dim else (size, 1)
    return ((iota(shape, dim) // most) * SLAB).astype(jnp.float32)


def message(ranks, dest, mine, place):
    size, dests = ranks.shape
    rank = nn(ranks, iota((dests, 8), 0) == dest)[:, :1]
    lane = iota((size, 128), 1)
    slots = (rank == (lane + 1).astype(jnp.float32)) & mine
    return nn(jnp.broadcast_to(place, (8, size)), slots)[:1]


def table_of(rows, flag):
    sub, lane = iota((8, 128), 0), iota((8, 128), 1)
    table = jnp.where((sub == 3) & (lane == 0), flag, 0.0)
    for n, values in enumerate(rows):
        table = jnp.where(sub == n, values, table)
    return table.astype(jnp.int32)


def left_kernel(at, x_rows, x_cols, y_rows, y_cols, z_rows, z_cols, send, positions):
    row, col = at[0], at[1]
    x, b = col >> 2, col & 3
    n = SIDE * x_rows.shape[-1]
    left_i = to_col(slab(x_rows, row))
    left_k = to_col(slab(x_cols, row)) + start_of(n, x_rows.shape[-1], 0)

    def needed(rows, cols, out_rows, out_cols):
        most = rows.shape[-1]
        outs = out_rows.shape[-1]
        keys = flat(rows, True) + start_of(SIDE * most, most, 1)
        others = flat(cols, True)
        out_i = out_rows[row].astype(jnp.float32)
        out_j = nt(eye(outs), out_cols[row])
        result = jnp.zeros((n, SIDE), jnp.float32)
        for c in range(SIDE):
            same_k = left_k == keys[c : c + 1]
            same_j = out_j[:, c : c + 1] == others[c : c + 1]
            hit = (nt(same_k, same_j) > 0.5) & (left_i == out_i[c : c + 1])
            some = jnp.max(hit.astype(jnp.float32), axis=1, keepdims=True)
            result = jnp.where(iota((n, SIDE), 1) == c, some, result)
        return result

    for_y = needed(x_rows, x_cols, y_rows, y_cols)
    for_z = needed(y_rows, y_cols, z_rows, z_cols) * (1.0 - for_y)
    group = iota((n, n), 0) >> 3 & 3
    same = group == (iota((n, n), 1) >> 3 & 3)
    before = same & (iota((n, n), 1) <= iota((n, n), 0))
    total_y, total_z = nn(same, for_y), nn(same, for_z)
    ranks = jnp.where(
        for_y > 0.5, nn(before, for_y), jnp.where(for_z > 0.5, total_y + nn(before, for_z), 0.0)
    )
    crosses = (iota((n, SIDE), 0) >> 3 & 3) != (iota((n, SIDE), 1) & 3)
    over = crosses & ((total_y > LEFT_FIRST) | (total_y + total_z > LEFT_ALL))
    flag = jnp.max(over.astype(jnp.float32))

    lane = iota((1, n), 1)
    place = (ring_piece((lane >> 5) - x & 3) * 8 + (lane & 7)).astype(jnp.float32)
    mine = (iota((n, 1), 0) >> 3 & 3) == b
    rows = [message(ranks, (x << 2) + (b ^ d), mine, place) for d in (1, 2, 3)]
    send[...] = table_of(rows, flag)
    rank = nt(iota((8, SIDE), 1) == col, ranks)[:1]
    d = (lane >> 3 & 3) ^ b
    spot = jnp.where(d == 0, place, (d * MOST).astype(jnp.float32) + jnp.maximum(rank - 1.0, 0.0))
    positions[...] = jnp.broadcast_to(spot, (8, n)).astype(jnp.int32)


def terms_list(out_i, out_j, left_i, left_k, left_pos, right_k, right_j, right_pos):
    outs, size = out_i.shape[0], left_i.shape[1]
    found = nt(jnp.where(out_j == right_j, right_pos + 1.0, 0.0), left_k == right_k)
    hit = (out_i == left_i) & (found > 0.5)
    marks = hit.astype(jnp.float32)
    rank = nn(marks, iota((size, size), 0) <= iota((size, size), 1))
    code = left_pos * 256.0 + (found - 1.0)
    lane = iota((outs, 128), 1)
    table = jnp.where(lane == COUNT, jnp.sum(marks, axis=1, keepdims=True), 0.0)
    for q in range(TERMS):
        picked = jnp.where(hit & (rank == q + 1.0), code, 0.0)
        table = table + jnp.where(lane == q, jnp.sum(picked, axis=1, keepdims=True), 0.0)
    multi = (jnp.sum(marks, axis=1, keepdims=True) > 1.5).astype(jnp.float32)
    multi = jnp.broadcast_to(multi, (outs, 128))
    order = nn(iota((outs, outs), 1) <= iota((outs, outs), 0), multi)
    slots = (multi > 0.5) & (order == (lane - (MULTI - 1)).astype(jnp.float32))
    entries = nn(iota((8, outs), 1), slots)[:1]
    entries = entries + jnp.where(lane[:1] == MULTIS, jnp.sum(multi, axis=0, keepdims=True), 0.0)
    table = table + jnp.where(iota((outs, 128), 0) == 0, entries, 0.0)
    return table, lane


def right_kernel(
    at, left_send, positions, x_rows, x_cols, y_rows, y_cols, z_rows, z_cols, send, y_plan, z_plan
):
    row, col = at[0], at[1]
    z, y, k = row >> 3, row >> 1 & 3, row & 1
    most, y_most, z_most = x_rows.shape[-1], y_rows.shape[-1], z_rows.shape[-1]
    n, m = SIDE * most, SIDE * y_most
    rows_i = flat(x_rows, False)
    rows_k = flat(x_cols, False) + start_of(n, most, 1)
    y_i = pick_row(flat(y_rows, True), col)[:1]
    y_j = pick_row(flat(y_cols, True), col)[:1]
    key = to_col(y_i) + start_of(m, y_most, 0)
    other = to_col(y_j)
    tile = iota((SIDE, SIDE * SIDE), 1)
    ours = (tile >> 4 == iota((SIDE, SIDE * SIDE), 0)) & ((tile & 15) == col)
    z_i = nn(ours, z_rows[...].reshape(SIDE * SIDE, z_most))
    z_j = nn(ours, z_cols[...].reshape(SIDE * SIDE, z_most))
    z_t = nt(eye(z_most), z_i)
    need = jnp.zeros((m, SIDE), jnp.float32)
    for r in range(SIDE):
        same_k = key == rows_k[r : r + 1]
        same_i = z_t[:, r : r + 1] == rows_i[r : r + 1]
        hit = (nt(same_k, same_i) > 0.5) & (other == z_j[r : r + 1])
        some = jnp.max(hit.astype(jnp.float32), axis=1, keepdims=True)
        need = jnp.where(iota((m, SIDE), 1) == r, some, need)
    need = nn(need, iota((SIDE, 8), 0) >> 1 == iota((SIDE, 8), 1)) > 0.5
    same = iota((m, m), 0) >> 4 == iota((m, m), 1) >> 4
    before = same & (iota((m, m), 1) <= iota((m, m), 0))
    ranks = jnp.where(need, nn(before, need), 0.0)
    crosses = (iota((m, 8), 0) >> 5 & 3) != (iota((m, 8), 1) & 3)
    over = crosses & (nn(same, need) > RIGHT_FIRST)
    flag = jnp.max(over.astype(jnp.float32))

    lane = iota((1, m), 1)
    slot = (lane & 15).astype(jnp.float32)
    tile = iota((m, 1), 0) >> 4
    dests = [(z << 2) + (y + d & 3) for d in (1, 3, 2)]
    rows = [message(ranks, dest, tile == row, slot) for dest in dests]
    send[:8] = table_of(rows, flag)
    rows = [message(ranks, dest, tile == (row ^ 8), slot) for dest in dests]
    send[8:] = table_of(rows, flag)
    rank = nt(iota((8, 8), 1) == row >> 1, ranks)[:1]
    piece = ring_piece((lane >> 5 & 3) - y & 3)
    spot = jnp.where(piece == 0, slot, jnp.maximum(rank - 1.0, 0.0))
    base = (lane >> 4 & 1 ^ k) * 128 + piece * MOST + (lane >> 7 ^ z) * 16
    y_pos = base.astype(jnp.float32) + spot
    lane = iota((1, n), 1)
    piece = ring_piece((lane >> 4 & 3) - y & 3)
    x_pos = (lane >> 3 & 1 ^ k) * 64 + piece * 16 + (lane >> 6 ^ z) * 8 + (lane & 7)
    x_pos = x_pos.astype(jnp.float32)

    x_k = pick_row(flat(x_rows, True), col)[:1] + start_of(n, most, 1)
    x_j = pick_row(flat(x_cols, True), col)[:1]
    left_i = slab(x_rows, row)
    left_k = to_col(slab(x_cols, row)) + start_of(n, most, 0)
    left_pos = positions[:1].astype(jnp.float32)

    def own(table):
        return pick_row(table[row], col)[:1]

    left_flag = left_send[3, 0].astype(jnp.float32)
    table, lane = terms_list(
        to_col(own(y_rows)), to_col(own(y_cols)), left_i, left_k, left_pos, x_k, x_j, x_pos
    )
    y_plan[...] = jnp.where(lane == FLAG, left_flag, table).astype(jnp.int32)
    out_i, out_j = to_col(own(z_rows)), to_col(own(z_cols))
    table, lane = terms_list(
        out_i, out_j, left_i, left_k, left_pos,
        y_i + start_of(m, y_most, 1), y_j, y_pos,
    )
    here = (own(x_rows) == out_i) & (own(x_cols) == out_j)
    slot = (iota(here.shape, 1) + 1).astype(jnp.float32)
    slot = jnp.sum(jnp.where(here, slot, 0.0), axis=1, keepdims=True)
    table = table + jnp.where(lane == OWN, slot, 0.0)
    table = jnp.where(lane == FLAG, left_flag + 2.0 * flag, table)
    z_plan[...] = table.astype(jnp.int32)


def pack_kernel(unit, count, parts, given, *refs):
    sources, outs = refs[:count], refs[count : count + len(parts)]
    held, table, in_sems, out_sems = refs[count + len(parts) :]
    loads = [pltpu.make_async_copy(given, table, in_sems.at[count])]
    loads += [
        pltpu.make_async_copy(source, held.at[pl.ds(n * unit, unit)], in_sems.at[n])
        for n, source in enumerate(sources)
    ]
    for load in loads:
        load.start()
    for load in loads:
        load.wait()
    copies = []
    for (row, first, last), out in zip(parts, outs):
        for n in range(last - first):
            copies.append(
                pltpu.make_async_copy(
                    held.at[table[row, first + n]], out.at[n], out_sems.at[len(copies)]
                )
            )
    for copy in copies:
        copy.start()
    for copy in copies:
        copy.wait()


def pack(table, sources, *parts):
    unit = sources[0].shape[0]
    sizes = [last - first for _, first, last in parts]
    return pl.pallas_call(
        functools.partial(pack_kernel, unit, len(sources), parts),
        out_shape=[jax.ShapeDtypeStruct((size, BLOCK, BLOCK), jnp.bfloat16) for size in sizes],
        in_specs=[pl.BlockSpec(memory_space=pl.ANY)] * (1 + len(sources)),
        out_specs=[pl.BlockSpec(memory_space=pl.ANY)] * len(sizes),
        scratch_shapes=[
            pltpu.VMEM((unit * len(sources), BLOCK, BLOCK), jnp.bfloat16),
            pltpu.SMEM(table.shape, jnp.int32),
            pltpu.SemaphoreType.DMA((len(sources) + 1,)),
            pltpu.SemaphoreType.DMA((sum(sizes),)),
        ],
    )(table, *sources)


def nothing(sizes):
    return pl.pallas_call(
        lambda *refs: None,
        out_shape=[jax.ShapeDtypeStruct((size, BLOCK, BLOCK), jnp.bfloat16) for size in sizes],
        out_specs=[pl.BlockSpec(memory_space=pl.ANY)] * len(sizes),
    )()


def products_kernel(layout, update, given, *refs):
    pieces = refs[: len(layout)]
    out, left, right, plan, sems = refs[len(layout) :]
    fetch = pltpu.make_async_copy(given, plan, sems.at[len(layout)])
    fetch.start()

    def copy(n):
        side, at, skip, size, _ = layout[n]
        buffer = (left, right)[side]
        source = pieces[n] if skip is None else pieces[n].at[pl.ds(skip, size)]
        return pltpu.make_async_copy(source, buffer.at[pl.ds(at, size)], sems.at[n])

    def each(act, flagged):
        for n, piece in enumerate(layout):
            if (piece[4] > 0) != flagged:
                continue
            if flagged:

                @pl.when(flag & piece[4] != 0)
                def _():
                    act(copy(n))

            else:
                act(copy(n))

    each(lambda c: c.start(), False)
    fetch.wait()
    flag = plan[0, FLAG]

    @pl.when(flag > 0)
    def _():
        each(lambda c: c.start(), True)
        each(lambda c: c.wait(), True)

    each(lambda c: c.wait(), False)

    def product(t, q):
        code = plan[t, q]
        return jnp.dot(
            left[code >> 8], right[code & 255], preferred_element_type=jnp.float32
        )

    def write(t, value):
        if update:
            slot = plan[t, OWN]
            x_here = left[jnp.maximum(slot - 1, 0)].astype(jnp.float32)
            value = 1.5 * jnp.where(slot > 0, x_here, 0.0) - 0.5 * value
        out[t] = value.astype(jnp.bfloat16)

    for t in range(out.shape[0]):
        write(t, jnp.where(plan[t, COUNT] > 0, product(t, 0), 0.0))

    def again(n, carry):
        t = plan[0, MULTI + n]
        terms = plan[t, COUNT]
        write(t, lax.fori_loop(1, terms, lambda q, total: total + product(t, q), product(t, 0)))
        return carry

    lax.fori_loop(0, plan[0, MULTIS], again, 0)


def products(plan, pieces, sizes, update):
    outs = plan.shape[0]
    layout = [
        (side, at, skip, p.shape[0] - (skip or 0), bit) for side, at, skip, bit, p in pieces
    ]
    return pl.pallas_call(
        functools.partial(products_kernel, layout, update),
        out_shape=jax.ShapeDtypeStruct((outs, BLOCK, BLOCK), jnp.bfloat16),
        in_specs=[pl.BlockSpec(memory_space=pl.ANY)] * (1 + len(pieces)),
        out_specs=pl.BlockSpec(memory_space=pltpu.VMEM),
        scratch_shapes=[
            pltpu.VMEM((sizes[0], BLOCK, BLOCK), jnp.bfloat16),
            pltpu.VMEM((sizes[1], BLOCK, BLOCK), jnp.bfloat16),
            pltpu.SMEM(plan.shape, jnp.int32),
            pltpu.SemaphoreType.DMA((len(pieces) + 1,)),
        ],
        compiler_params=pltpu.CompilerParams(vmem_limit_bytes=32 * 1024 * 1024),
    )(plan, *[p[-1] for p in pieces])


def row_send(blocks, perm):
    return lax.ppermute(blocks, "row", perm)


def col_send(blocks, perm):
    return lax.ppermute(blocks, "col", perm)


def after(value, *others):
    return lax.optimization_barrier((value, others))[0]


def shards(x_blocks, x_rows, x_cols, y_rows, y_cols, z_rows, z_cols):
    row = lax.axis_index("row")
    col = lax.axis_index("col")
    at = jnp.stack([row, col]).astype(jnp.int32)
    tables = (x_rows, x_cols, y_rows, y_cols, z_rows, z_cols)
    tile = x_blocks[0, 0]
    y_most, z_most = y_rows.shape[-1], z_rows.shape[-1]
    smem = pl.BlockSpec(memory_space=pltpu.SMEM)
    vmem = pl.BlockSpec(memory_space=pltpu.VMEM)

    far = row_send(tile, Z_SWAP)
    near = [col_send(tile, ring) for ring in X_RING]
    left_send, positions = pl.pallas_call(
        left_kernel,
        out_shape=(jax.ShapeDtypeStruct((8, 128), jnp.int32),) * 2,
        in_specs=[smem] + [vmem] * 6,
    )(at, *tables)
    near, left_send, positions = lax.optimization_barrier((near, left_send, positions))
    quad = [tile] + near
    ends = (LEFT_FIRST, LEFT_ALL, LEFT_FIRST)
    parts = [(d, 0, end) for d, end in enumerate(ends)]
    parts += [(d, LEFT_FIRST, LEFT_ALL) for d in (0, 2)]
    first = pack(left_send, quad, *parts)
    first, far = lax.optimization_barrier((first, far))
    first, second = first[:3], first[3:]
    one, two = [col_send(blocks, swap) for blocks, swap in zip(first[:2], B_SWAP[:2])]
    first = [one, two, col_send(after(first[2], one), B_SWAP[2])]
    pair = jnp.concatenate([tile, far])
    across, up, down = [row_send(pair, Y_RING[n]) for n in (2, 0, 1)]
    right_send, y_plan, z_plan = pl.pallas_call(
        right_kernel,
        out_shape=(
            jax.ShapeDtypeStruct((16, 128), jnp.int32),
            jax.ShapeDtypeStruct((y_most, 128), jnp.int32),
            jax.ShapeDtypeStruct((z_most, 128), jnp.int32),
        ),
        in_specs=[smem, smem] + [vmem] * 7,
    )(at, left_send, positions, *tables)
    first, up, down, across, right_send, y_plan, z_plan = lax.optimization_barrier(
        (first, up, down, across, right_send, y_plan, z_plan)
    )
    x_half = [pair, up, down, across]
    x_mate = [row_send(blocks, CORE_SWAP) for blocks in x_half]

    def more_left():
        rest = pack(left_send, quad, *[(d, end, MOST) for d, end in enumerate(ends)])
        return tuple(col_send(blocks, swap) for blocks, swap in zip(rest, B_SWAP))

    rest = lax.cond(
        left_send[3, 0] > 0, more_left, lambda: tuple(nothing([MOST - end for end in ends]))
    )

    left = [(0, 8 * n, None, 0, p) for n, p in enumerate(quad)]
    left += [(0, MOST * (n + 1), None, 0, p) for n, p in enumerate(first)]
    right = [(1, 16 * n, None, 0, p) for n, p in enumerate(x_half + x_mate)]
    extra = [(0, MOST * (n + 1) + end, None, 1, p) for n, (end, p) in enumerate(zip(ends, rest))]
    y_tile = products(y_plan, left + right + extra, (4 * MOST, 128), False)

    y_far = row_send(y_tile, Z_SWAP)
    tile_mate = row_send(y_tile, CORE_SWAP)
    own_send = pack(right_send, [y_tile], *[(d, 0, RIGHT_FIRST) for d in range(3)])
    own_near = [row_send(blocks, ring) for blocks, ring in zip(own_send, Y_RING)]
    y_far, tile_mate, own_near = lax.optimization_barrier((y_far, tile_mate, own_near))
    own_mate = [row_send(blocks, CORE_SWAP) for blocks in own_near]
    far_send = pack(right_send, [y_far], *[(8 + d, 0, RIGHT_FIRST) for d in range(3)])
    far_mate = row_send(y_far, CORE_SWAP)
    far_send, far_mate, own_mate, second = lax.optimization_barrier(
        (far_send, far_mate, own_mate, second)
    )
    far_near = [row_send(blocks, ring) for blocks, ring in zip(far_send, Y_RING)]
    second = [col_send(blocks, swap) for blocks, swap in zip(second, B_SWAP[::2])]
    far_near, second = lax.optimization_barrier((far_near, second))
    far_near_mate = [row_send(blocks, CORE_SWAP) for blocks in far_near]

    def more_right():
        blocks = pack(right_send, [y_tile], *[(d, RIGHT_FIRST, y_most) for d in range(3)])
        blocks += pack(right_send, [y_far], *[(8 + d, RIGHT_FIRST, y_most) for d in range(3)])
        blocks = [row_send(b, ring) for b, ring in zip(blocks, Y_RING + Y_RING)]
        return tuple(blocks + [row_send(b, CORE_SWAP) for b in blocks])

    more = lax.cond(
        right_send[3, 0] > 0, more_right, lambda: tuple(nothing([y_most - RIGHT_FIRST] * 12))
    )

    left += [(0, MOST * (2 * n + 1) + LEFT_FIRST, None, 0, p) for n, p in enumerate(second)]
    extra = [
        (0, MOST * (n + 1) + LEFT_ALL, LEFT_ALL - end, 1, p)
        for n, (end, p) in enumerate(zip(ends, rest))
    ]
    right = []
    spots = [i * MOST + j * y_most for i in range(4) for j in range(2)]
    ours = [y_tile, y_far] + [p for both in zip(own_near, far_near) for p in both]
    theirs = [tile_mate, far_mate] + [p for both in zip(own_mate, far_near_mate) for p in both]
    for n, side in enumerate((ours, theirs)):
        right += [(1, n * 128 + spot, None, 0, p) for spot, p in zip(spots, side)]
        rest_spots = spots[2::2] + spots[3::2]
        extra += [
            (1, n * 128 + spot + RIGHT_FIRST, None, 2, p)
            for spot, p in zip(rest_spots, more[6 * n : 6 * n + 6])
        ]
    update = products(z_plan, left + right + extra, (4 * MOST, 8 * MOST), True)
    return (y_tile[None, None], update[None, None])


def solution(mesh):
    in_specs = (P("row", "col", None, None, None), P(), P(), P(), P(), P(), P())
    out_specs = (P("row", "col", None, None, None), P("row", "col", None, None, None))
    return jax.shard_map(shards, mesh=mesh, in_specs=in_specs, out_specs=out_specs, check_vma=False)
```

```python
import functools

import jax
import jax.numpy as jnp
from jax import lax
from jax.experimental import pallas as pl
from jax.experimental.pallas import tpu as pltpu
from jax.sharding import PartitionSpec as P

SLAB = 32
SIDE = 16
BLOCK = 128
TERMS = 32
COUNT = 32
OWN = 33
FLAG = 34
MULTIS = 35
MULTI = 40
LEFT_FIRST = 10
LEFT_ALL = 17
RIGHT_FIRST = 10
MOST = 32

ROW = [(z, y, k) for z in range(2) for y in range(4) for k in range(2)]
COL = [(x, b) for x in range(4) for b in range(4)]


def row_at(z, y, k):
    return z * 8 + y % 4 * 2 + k


def col_at(x, b):
    return x % 4 * 4 + b


Z_SWAP = [(row_at(z, y, k), row_at(1 - z, y, k)) for z, y, k in ROW]
CORE_SWAP = [(row_at(z, y, k), row_at(z, y, 1 - k)) for z, y, k in ROW]
Y_RING = [[(row_at(z, y, k), row_at(z, y + d, k)) for z, y, k in ROW] for d in (1, 3, 2)]
X_RING = [[(col_at(x, b), col_at(x + d, b)) for x, b in COL] for d in (1, 3, 2)]
B_SWAP = [[(col_at(x, b), col_at(x, b ^ d)) for x, b in COL] for d in (1, 2, 3)]


def ring_piece(offset):
    return jnp.where(offset == 0, 0, jnp.where(offset == 1, 2, jnp.where(offset == 2, 3, 1)))


def iota(shape, dim):
    return lax.broadcasted_iota(jnp.int32, shape, dim)


def half(values):
    return values.astype(jnp.float32).astype(jnp.bfloat16)


def nn(a, b):
    return jnp.dot(half(a), half(b), preferred_element_type=jnp.float32)


def nt(a, b):
    return lax.dot_general(
        half(a), half(b), (((1,), (1,)), ((), ())), preferred_element_type=jnp.float32
    )


def eye(size):
    return iota((size, size), 0) == iota((size, size), 1)


def flat(table, by_col):
    most = table.shape[-1]
    size = SIDE * most
    values = table[...].reshape(SIDE * SIDE, most)
    wide = nn(values, (iota((most, size), 1) & (most - 1)) == iota((most, size), 0))
    tile = iota((SIDE * SIDE, size), 0)
    section = iota((SIDE * SIDE, size), 1) // most
    pick = iota((SIDE, SIDE * SIDE), 1)
    if by_col:
        wide = jnp.where(section == tile >> 4, wide, 0.0)
        pick = pick & 15
    else:
        wide = jnp.where(section == tile & 15, wide, 0.0)
        pick = pick >> 4
    return nn(pick == iota((SIDE, SIDE * SIDE), 0), wide)


def slab(table, row):
    most = table.shape[-1]
    size = SIDE * most
    wide = nn(table[row], (iota((most, size), 1) & (most - 1)) == iota((most, size), 0))
    wide = jnp.where(iota((SIDE, size), 1) // most == iota((SIDE, size), 0), wide, 0.0)
    return jnp.sum(wide, axis=0, keepdims=True)


def pick_row(values, index):
    return nn(iota((8, values.shape[0]), 1) == index, values)


def to_col(lanes):
    size = lanes.shape[1]
    return nt(eye(size), jnp.broadcast_to(lanes[:1], (8, size)))[:, :1]


def start_of(size, most, dim):
    shape = (1, size) if dim else (size, 1)
    return ((iota(shape, dim) // most) * SLAB).astype(jnp.float32)


def message(ranks, dest, mine, place):
    size, dests = ranks.shape
    rank = nn(ranks, iota((dests, 8), 0) == dest)[:, :1]
    lane = iota((size, 128), 1)
    slots = (rank == (lane + 1).astype(jnp.float32)) & mine
    return nn(jnp.broadcast_to(place, (8, size)), slots)[:1]


def table_of(rows, flag):
    sub, lane = iota((8, 128), 0), iota((8, 128), 1)
    table = jnp.where((sub == 3) & (lane == 0), flag, 0.0)
    for n, values in enumerate(rows):
        table = jnp.where(sub == n, values, table)
    return table.astype(jnp.int32)


def left_kernel(at, x_rows, x_cols, y_rows, y_cols, z_rows, z_cols, send, positions):
    row, col = at[0], at[1]
    x, b = col >> 2, col & 3
    n = SIDE * x_rows.shape[-1]
    left_i = to_col(slab(x_rows, row))
    left_k = to_col(slab(x_cols, row)) + start_of(n, x_rows.shape[-1], 0)

    def needed(rows, cols, out_rows, out_cols):
        most = rows.shape[-1]
        outs = out_rows.shape[-1]
        keys = flat(rows, True) + start_of(SIDE * most, most, 1)
        others = flat(cols, True)
        out_i = out_rows[row].astype(jnp.float32)
        out_j = nt(eye(outs), out_cols[row])
        result = jnp.zeros((n, SIDE), jnp.float32)
        for c in range(SIDE):
            same_k = left_k == keys[c : c + 1]
            same_j = out_j[:, c : c + 1] == others[c : c + 1]
            hit = (nt(same_k, same_j) > 0.5) & (left_i == out_i[c : c + 1])
            some = jnp.max(hit.astype(jnp.float32), axis=1, keepdims=True)
            result = jnp.where(iota((n, SIDE), 1) == c, some, result)
        return result

    for_y = needed(x_rows, x_cols, y_rows, y_cols)
    for_z = needed(y_rows, y_cols, z_rows, z_cols) * (1.0 - for_y)
    group = iota((n, n), 0) >> 3 & 3
    same = group == (iota((n, n), 1) >> 3 & 3)
    before = same & (iota((n, n), 1) <= iota((n, n), 0))
    total_y, total_z = nn(same, for_y), nn(same, for_z)
    ranks = jnp.where(
        for_y > 0.5, nn(before, for_y), jnp.where(for_z > 0.5, total_y + nn(before, for_z), 0.0)
    )
    crosses = (iota((n, SIDE), 0) >> 3 & 3) != (iota((n, SIDE), 1) & 3)
    over = crosses & ((total_y > LEFT_FIRST) | (total_y + total_z > LEFT_ALL))
    flag = jnp.max(over.astype(jnp.float32))

    lane = iota((1, n), 1)
    place = (ring_piece((lane >> 5) - x & 3) * 8 + (lane & 7)).astype(jnp.float32)
    mine = (iota((n, 1), 0) >> 3 & 3) == b
    rows = [message(ranks, (x << 2) + (b ^ d), mine, place) for d in (1, 2, 3)]
    send[...] = table_of(rows, flag)
    rank = nt(iota((8, SIDE), 1) == col, ranks)[:1]
    d = (lane >> 3 & 3) ^ b
    spot = jnp.where(d == 0, place, (d * MOST).astype(jnp.float32) + jnp.maximum(rank - 1.0, 0.0))
    positions[...] = jnp.broadcast_to(spot, (8, n)).astype(jnp.int32)


def terms_list(out_i, out_j, left_i, left_k, left_pos, right_k, right_j, right_pos):
    outs, size = out_i.shape[0], left_i.shape[1]
    found = nt(jnp.where(out_j == right_j, right_pos + 1.0, 0.0), left_k == right_k)
    hit = (out_i == left_i) & (found > 0.5)
    marks = hit.astype(jnp.float32)
    rank = nn(marks, iota((size, size), 0) <= iota((size, size), 1))
    code = left_pos * 256.0 + (found - 1.0)
    lane = iota((outs, 128), 1)
    table = jnp.where(lane == COUNT, jnp.sum(marks, axis=1, keepdims=True), 0.0)
    for q in range(TERMS):
        picked = jnp.where(hit & (rank == q + 1.0), code, 0.0)
        table = table + jnp.where(lane == q, jnp.sum(picked, axis=1, keepdims=True), 0.0)
    multi = (jnp.sum(marks, axis=1, keepdims=True) > 1.5).astype(jnp.float32)
    multi = jnp.broadcast_to(multi, (outs, 128))
    order = nn(iota((outs, outs), 1) <= iota((outs, outs), 0), multi)
    slots = (multi > 0.5) & (order == (lane - (MULTI - 1)).astype(jnp.float32))
    entries = nn(iota((8, outs), 1), slots)[:1]
    entries = entries + jnp.where(lane[:1] == MULTIS, jnp.sum(multi, axis=0, keepdims=True), 0.0)
    table = table + jnp.where(iota((outs, 128), 0) == 0, entries, 0.0)
    return table, lane


def right_kernel(
    at, left_send, positions, x_rows, x_cols, y_rows, y_cols, z_rows, z_cols, send, y_plan, z_plan
):
    row, col = at[0], at[1]
    z, y, k = row >> 3, row >> 1 & 3, row & 1
    most, y_most, z_most = x_rows.shape[-1], y_rows.shape[-1], z_rows.shape[-1]
    n, m = SIDE * most, SIDE * y_most
    rows_i = flat(x_rows, False)
    rows_k = flat(x_cols, False) + start_of(n, most, 1)
    y_i = pick_row(flat(y_rows, True), col)[:1]
    y_j = pick_row(flat(y_cols, True), col)[:1]
    key = to_col(y_i) + start_of(m, y_most, 0)
    other = to_col(y_j)
    tile = iota((SIDE, SIDE * SIDE), 1)
    ours = (tile >> 4 == iota((SIDE, SIDE * SIDE), 0)) & ((tile & 15) == col)
    z_i = nn(ours, z_rows[...].reshape(SIDE * SIDE, z_most))
    z_j = nn(ours, z_cols[...].reshape(SIDE * SIDE, z_most))
    z_t = nt(eye(z_most), z_i)
    need = jnp.zeros((m, SIDE), jnp.float32)
    for r in range(SIDE):
        same_k = key == rows_k[r : r + 1]
        same_i = z_t[:, r : r + 1] == rows_i[r : r + 1]
        hit = (nt(same_k, same_i) > 0.5) & (other == z_j[r : r + 1])
        some = jnp.max(hit.astype(jnp.float32), axis=1, keepdims=True)
        need = jnp.where(iota((m, SIDE), 1) == r, some, need)
    need = nn(need, iota((SIDE, 8), 0) >> 1 == iota((SIDE, 8), 1)) > 0.5
    same = iota((m, m), 0) >> 4 == iota((m, m), 1) >> 4
    before = same & (iota((m, m), 1) <= iota((m, m), 0))
    ranks = jnp.where(need, nn(before, need), 0.0)
    crosses = (iota((m, 8), 0) >> 5 & 3) != (iota((m, 8), 1) & 3)
    over = crosses & (nn(same, need) > RIGHT_FIRST)
    flag = jnp.max(over.astype(jnp.float32))

    lane = iota((1, m), 1)
    slot = (lane & 15).astype(jnp.float32)
    tile = iota((m, 1), 0) >> 4
    dests = [(z << 2) + (y + d & 3) for d in (1, 3, 2)]
    rows = [message(ranks, dest, tile == row, slot) for dest in dests]
    send[:8] = table_of(rows, flag)
    rows = [message(ranks, dest, tile == (row ^ 8), slot) for dest in dests]
    send[8:] = table_of(rows, flag)
    rank = nt(iota((8, 8), 1) == row >> 1, ranks)[:1]
    piece = ring_piece((lane >> 5 & 3) - y & 3)
    spot = jnp.where(piece == 0, slot, jnp.maximum(rank - 1.0, 0.0))
    base = (lane >> 4 & 1 ^ k) * 128 + piece * MOST + (lane >> 7 ^ z) * 16
    y_pos = base.astype(jnp.float32) + spot
    lane = iota((1, n), 1)
    piece = ring_piece((lane >> 4 & 3) - y & 3)
    x_pos = (lane >> 3 & 1 ^ k) * 64 + piece * 16 + (lane >> 6 ^ z) * 8 + (lane & 7)
    x_pos = x_pos.astype(jnp.float32)

    x_k = pick_row(flat(x_rows, True), col)[:1] + start_of(n, most, 1)
    x_j = pick_row(flat(x_cols, True), col)[:1]
    left_i = slab(x_rows, row)
    left_k = to_col(slab(x_cols, row)) + start_of(n, most, 0)
    left_pos = positions[:1].astype(jnp.float32)

    def own(table):
        return pick_row(table[row], col)[:1]

    left_flag = left_send[3, 0].astype(jnp.float32)
    table, lane = terms_list(
        to_col(own(y_rows)), to_col(own(y_cols)), left_i, left_k, left_pos, x_k, x_j, x_pos
    )
    y_plan[...] = jnp.where(lane == FLAG, left_flag, table).astype(jnp.int32)
    out_i, out_j = to_col(own(z_rows)), to_col(own(z_cols))
    table, lane = terms_list(
        out_i, out_j, left_i, left_k, left_pos,
        y_i + start_of(m, y_most, 1), y_j, y_pos,
    )
    here = (own(x_rows) == out_i) & (own(x_cols) == out_j)
    slot = (iota(here.shape, 1) + 1).astype(jnp.float32)
    slot = jnp.sum(jnp.where(here, slot, 0.0), axis=1, keepdims=True)
    table = table + jnp.where(lane == OWN, slot, 0.0)
    table = jnp.where(lane == FLAG, left_flag + 2.0 * flag, table)
    z_plan[...] = table.astype(jnp.int32)


def pack_kernel(unit, count, parts, given, *refs):
    sources, outs = refs[:count], refs[count : count + len(parts)]
    held, table, in_sems, out_sems = refs[count + len(parts) :]
    loads = [pltpu.make_async_copy(given, table, in_sems.at[count])]
    loads += [
        pltpu.make_async_copy(source, held.at[pl.ds(n * unit, unit)], in_sems.at[n])
        for n, source in enumerate(sources)
    ]
    for load in loads:
        load.start()
    for load in loads:
        load.wait()
    copies = []
    for (row, first, last), out in zip(parts, outs):
        for n in range(last - first):
            copies.append(
                pltpu.make_async_copy(
                    held.at[table[row, first + n]], out.at[n], out_sems.at[len(copies)]
                )
            )
    for copy in copies:
        copy.start()
    for copy in copies:
        copy.wait()


def pack(table, sources, *parts):
    unit = sources[0].shape[0]
    sizes = [last - first for _, first, last in parts]
    return pl.pallas_call(
        functools.partial(pack_kernel, unit, len(sources), parts),
        out_shape=[jax.ShapeDtypeStruct((size, BLOCK, BLOCK), jnp.bfloat16) for size in sizes],
        in_specs=[pl.BlockSpec(memory_space=pl.ANY)] * (1 + len(sources)),
        out_specs=[pl.BlockSpec(memory_space=pl.ANY)] * len(sizes),
        scratch_shapes=[
            pltpu.VMEM((unit * len(sources), BLOCK, BLOCK), jnp.bfloat16),
            pltpu.SMEM(table.shape, jnp.int32),
            pltpu.SemaphoreType.DMA((len(sources) + 1,)),
            pltpu.SemaphoreType.DMA((sum(sizes),)),
        ],
    )(table, *sources)


def nothing(sizes):
    return pl.pallas_call(
        lambda *refs: None,
        out_shape=[jax.ShapeDtypeStruct((size, BLOCK, BLOCK), jnp.bfloat16) for size in sizes],
        out_specs=[pl.BlockSpec(memory_space=pl.ANY)] * len(sizes),
    )()


def products_kernel(layout, update, given, *refs):
    pieces = refs[: len(layout)]
    out, left, right, plan, sems = refs[len(layout) :]
    fetch = pltpu.make_async_copy(given, plan, sems.at[len(layout)])
    fetch.start()

    def copy(n):
        side, at, skip, size, _ = layout[n]
        buffer = (left, right)[side]
        source = pieces[n] if skip is None else pieces[n].at[pl.ds(skip, size)]
        return pltpu.make_async_copy(source, buffer.at[pl.ds(at, size)], sems.at[n])

    def each(act, flagged):
        for n, piece in enumerate(layout):
            if (piece[4] > 0) != flagged:
                continue
            if flagged:

                @pl.when(flag & piece[4] != 0)
                def _():
                    act(copy(n))

            else:
                act(copy(n))

    each(lambda c: c.start(), False)
    fetch.wait()
    flag = plan[0, FLAG]

    @pl.when(flag > 0)
    def _():
        each(lambda c: c.start(), True)
        each(lambda c: c.wait(), True)

    each(lambda c: c.wait(), False)

    def product(t, q):
        code = plan[t, q]
        return jnp.dot(
            left[code >> 8], right[code & 255], preferred_element_type=jnp.float32
        )

    def write(t, value):
        if update:
            slot = plan[t, OWN]
            x_here = left[jnp.maximum(slot - 1, 0)].astype(jnp.float32)
            value = 1.5 * jnp.where(slot > 0, x_here, 0.0) - 0.5 * value
        out[t] = value.astype(jnp.bfloat16)

    for t in range(out.shape[0]):
        write(t, jnp.where(plan[t, COUNT] > 0, product(t, 0), 0.0))

    def again(n, carry):
        t = plan[0, MULTI + n]
        terms = plan[t, COUNT]
        write(t, lax.fori_loop(1, terms, lambda q, total: total + product(t, q), product(t, 0)))
        return carry

    lax.fori_loop(0, plan[0, MULTIS], again, 0)


def products(plan, pieces, sizes, update):
    outs = plan.shape[0]
    layout = [
        (side, at, skip, p.shape[0] - (skip or 0), bit) for side, at, skip, bit, p in pieces
    ]
    return pl.pallas_call(
        functools.partial(products_kernel, layout, update),
        out_shape=jax.ShapeDtypeStruct((outs, BLOCK, BLOCK), jnp.bfloat16),
        in_specs=[pl.BlockSpec(memory_space=pl.ANY)] * (1 + len(pieces)),
        out_specs=pl.BlockSpec(memory_space=pltpu.VMEM),
        scratch_shapes=[
            pltpu.VMEM((sizes[0], BLOCK, BLOCK), jnp.bfloat16),
            pltpu.VMEM((sizes[1], BLOCK, BLOCK), jnp.bfloat16),
            pltpu.SMEM(plan.shape, jnp.int32),
            pltpu.SemaphoreType.DMA((len(pieces) + 1,)),
        ],
        compiler_params=pltpu.CompilerParams(vmem_limit_bytes=32 * 1024 * 1024),
    )(plan, *[p[-1] for p in pieces])


def row_send(blocks, perm):
    return lax.ppermute(blocks, "row", perm)


def col_send(blocks, perm):
    return lax.ppermute(blocks, "col", perm)


def after(value, *others):
    return lax.optimization_barrier((value, others))[0]


def shards(x_blocks, x_rows, x_cols, y_rows, y_cols, z_rows, z_cols):
    row = lax.axis_index("row")
    col = lax.axis_index("col")
    at = jnp.stack([row, col]).astype(jnp.int32)
    tables = (x_rows, x_cols, y_rows, y_cols, z_rows, z_cols)
    tile = x_blocks[0, 0]
    y_most, z_most = y_rows.shape[-1], z_rows.shape[-1]
    smem = pl.BlockSpec(memory_space=pltpu.SMEM)
    vmem = pl.BlockSpec(memory_space=pltpu.VMEM)

    far = row_send(tile, Z_SWAP)
    near = [col_send(tile, ring) for ring in X_RING]
    left_send, positions = pl.pallas_call(
        left_kernel,
        out_shape=(jax.ShapeDtypeStruct((8, 128), jnp.int32),) * 2,
        in_specs=[smem] + [vmem] * 6,
    )(at, *tables)
    near, left_send, positions = lax.optimization_barrier((near, left_send, positions))
    quad = [tile] + near
    ends = (LEFT_FIRST, LEFT_ALL, LEFT_FIRST)
    parts = [(d, 0, end) for d, end in enumerate(ends)]
    parts += [(d, LEFT_FIRST, LEFT_ALL) for d in (0, 2)]
    first = pack(left_send, quad, *parts)
    first, second = first[:3], first[3:]
    one, two = [col_send(blocks, swap) for blocks, swap in zip(first[:2], B_SWAP[:2])]
    first = [one, two, col_send(after(first[2], one), B_SWAP[2])]
    pair = jnp.concatenate([tile, far])
    across, up, down = [row_send(pair, Y_RING[n]) for n in (2, 0, 1)]
    right_send, y_plan, z_plan = pl.pallas_call(
        right_kernel,
        out_shape=(
            jax.ShapeDtypeStruct((16, 128), jnp.int32),
            jax.ShapeDtypeStruct((y_most, 128), jnp.int32),
            jax.ShapeDtypeStruct((z_most, 128), jnp.int32),
        ),
        in_specs=[smem, smem] + [vmem] * 7,
    )(at, left_send, positions, *tables)
    first, up, down, across, right_send, y_plan, z_plan = lax.optimization_barrier(
        (first, up, down, across, right_send, y_plan, z_plan)
    )
    x_half = [pair, up, down, across]
    x_mate = [row_send(blocks, CORE_SWAP) for blocks in x_half]

    def more_left():
        rest = pack(left_send, quad, *[(d, end, MOST) for d, end in enumerate(ends)])
        return tuple(col_send(blocks, swap) for blocks, swap in zip(rest, B_SWAP))

    rest = lax.cond(
        left_send[3, 0] > 0, more_left, lambda: tuple(nothing([MOST - end for end in ends]))
    )

    left = [(0, 8 * n, None, 0, p) for n, p in enumerate(quad)]
    left += [(0, MOST * (n + 1), None, 0, p) for n, p in enumerate(first)]
    right = [(1, 16 * n, None, 0, p) for n, p in enumerate(x_half + x_mate)]
    extra = [(0, MOST * (n + 1) + end, None, 1, p) for n, (end, p) in enumerate(zip(ends, rest))]
    y_tile = products(y_plan, left + right + extra, (4 * MOST, 128), False)

    y_far = row_send(y_tile, Z_SWAP)
    tile_mate = row_send(y_tile, CORE_SWAP)
    own_send = pack(right_send, [y_tile], *[(d, 0, RIGHT_FIRST) for d in range(3)])
    own_near = [row_send(blocks, ring) for blocks, ring in zip(own_send, Y_RING)]
    y_far, tile_mate, own_near = lax.optimization_barrier((y_far, tile_mate, own_near))
    own_mate = [row_send(blocks, CORE_SWAP) for blocks in own_near]
    far_send = pack(right_send, [y_far], *[(8 + d, 0, RIGHT_FIRST) for d in range(3)])
    far_mate = row_send(y_far, CORE_SWAP)
    far_send, far_mate, own_mate, second = lax.optimization_barrier(
        (far_send, far_mate, own_mate, second)
    )
    far_near = [row_send(blocks, ring) for blocks, ring in zip(far_send, Y_RING)]
    second = [col_send(blocks, swap) for blocks, swap in zip(second, B_SWAP[::2])]
    far_near, second = lax.optimization_barrier((far_near, second))
    far_near_mate = [row_send(blocks, CORE_SWAP) for blocks in far_near]

    def more_right():
        blocks = pack(right_send, [y_tile], *[(d, RIGHT_FIRST, y_most) for d in range(3)])
        blocks += pack(right_send, [y_far], *[(8 + d, RIGHT_FIRST, y_most) for d in range(3)])
        blocks = [row_send(b, ring) for b, ring in zip(blocks, Y_RING + Y_RING)]
        return tuple(blocks + [row_send(b, CORE_SWAP) for b in blocks])

    more = lax.cond(
        right_send[3, 0] > 0, more_right, lambda: tuple(nothing([y_most - RIGHT_FIRST] * 12))
    )

    left += [(0, MOST * (2 * n + 1) + LEFT_FIRST, None, 0, p) for n, p in enumerate(second)]
    extra = [
        (0, MOST * (n + 1) + LEFT_ALL, LEFT_ALL - end, 1, p)
        for n, (end, p) in enumerate(zip(ends, rest))
    ]
    right = []
    spots = [i * MOST + j * y_most for i in range(4) for j in range(2)]
    ours = [y_tile, y_far] + [p for both in zip(own_near, far_near) for p in both]
    theirs = [tile_mate, far_mate] + [p for both in zip(own_mate, far_near_mate) for p in both]
    for n, side in enumerate((ours, theirs)):
        right += [(1, n * 128 + spot, None, 0, p) for spot, p in zip(spots, side)]
        rest_spots = spots[2::2] + spots[3::2]
        extra += [
            (1, n * 128 + spot + RIGHT_FIRST, None, 2, p)
            for spot, p in zip(rest_spots, more[6 * n : 6 * n + 6])
        ]
    update = products(z_plan, left + right + extra, (4 * MOST, 8 * MOST), True)
    return (y_tile[None, None], update[None, None])


def solution(mesh):
    in_specs = (P("row", "col", None, None, None), P(), P(), P(), P(), P(), P())
    out_specs = (P("row", "col", None, None, None), P("row", "col", None, None, None))
    return jax.shard_map(shards, mesh=mesh, in_specs=in_specs, out_specs=out_specs, check_vma=False)
```

```python
import functools

import jax
import jax.numpy as jnp
from jax import lax
from jax.experimental import pallas as pl
from jax.experimental.pallas import tpu as pltpu
from jax.sharding import PartitionSpec as P

SLAB = 32
SIDE = 16
BLOCK = 128
TERMS = 32
COUNT = 32
OWN = 33
FLAG = 34
MULTIS = 35
MULTI = 40
LEFT_FIRST = 10
LEFT_ALL = 17
RIGHT_FIRST = 10
MOST = 32

ROW = [(z, y, k) for z in range(2) for y in range(4) for k in range(2)]
COL = [(x, b) for x in range(4) for b in range(4)]


def row_at(z, y, k):
    return z * 8 + y % 4 * 2 + k


def col_at(x, b):
    return x % 4 * 4 + b


Z_SWAP = [(row_at(z, y, k), row_at(1 - z, y, k)) for z, y, k in ROW]
CORE_SWAP = [(row_at(z, y, k), row_at(z, y, 1 - k)) for z, y, k in ROW]
Y_RING = [[(row_at(z, y, k), row_at(z, y + d, k)) for z, y, k in ROW] for d in (1, 3, 2)]
X_RING = [[(col_at(x, b), col_at(x + d, b)) for x, b in COL] for d in (1, 3, 2)]
B_SWAP = [[(col_at(x, b), col_at(x, b ^ d)) for x, b in COL] for d in (1, 2, 3)]


def ring_piece(offset):
    return jnp.where(offset == 0, 0, jnp.where(offset == 1, 2, jnp.where(offset == 2, 3, 1)))


def iota(shape, dim):
    return lax.broadcasted_iota(jnp.int32, shape, dim)


def half(values):
    return values.astype(jnp.float32).astype(jnp.bfloat16)


def nn(a, b):
    return jnp.dot(half(a), half(b), preferred_element_type=jnp.float32)


def nt(a, b):
    return lax.dot_general(
        half(a), half(b), (((1,), (1,)), ((), ())), preferred_element_type=jnp.float32
    )


def eye(size):
    return iota((size, size), 0) == iota((size, size), 1)


def flat(table, by_col):
    most = table.shape[-1]
    size = SIDE * most
    values = table[...].reshape(SIDE * SIDE, most)
    wide = nn(values, (iota((most, size), 1) & (most - 1)) == iota((most, size), 0))
    tile = iota((SIDE * SIDE, size), 0)
    section = iota((SIDE * SIDE, size), 1) // most
    pick = iota((SIDE, SIDE * SIDE), 1)
    if by_col:
        wide = jnp.where(section == tile >> 4, wide, 0.0)
        pick = pick & 15
    else:
        wide = jnp.where(section == tile & 15, wide, 0.0)
        pick = pick >> 4
    return nn(pick == iota((SIDE, SIDE * SIDE), 0), wide)


def slab(table, row):
    most = table.shape[-1]
    size = SIDE * most
    wide = nn(table[row], (iota((most, size), 1) & (most - 1)) == iota((most, size), 0))
    wide = jnp.where(iota((SIDE, size), 1) // most == iota((SIDE, size), 0), wide, 0.0)
    return jnp.sum(wide, axis=0, keepdims=True)


def pick_row(values, index):
    return nn(iota((8, values.shape[0]), 1) == index, values)


def to_col(lanes):
    size = lanes.shape[1]
    return nt(eye(size), jnp.broadcast_to(lanes[:1], (8, size)))[:, :1]


def start_of(size, most, dim):
    shape = (1, size) if dim else (size, 1)
    return ((iota(shape, dim) // most) * SLAB).astype(jnp.float32)


def message(ranks, dest, mine, place):
    size, dests = ranks.shape
    rank = nn(ranks, iota((dests, 8), 0) == dest)[:, :1]
    lane = iota((size, 128), 1)
    slots = (rank == (lane + 1).astype(jnp.float32)) & mine
    return nn(jnp.broadcast_to(place, (8, size)), slots)[:1]


def table_of(rows, flag):
    sub, lane = iota((8, 128), 0), iota((8, 128), 1)
    table = jnp.where((sub == 3) & (lane == 0), flag, 0.0)
    for n, values in enumerate(rows):
        table = jnp.where(sub == n, values, table)
    return table.astype(jnp.int32)


def left_kernel(at, x_rows, x_cols, y_rows, y_cols, z_rows, z_cols, send, positions):
    row, col = at[0], at[1]
    x, b = col >> 2, col & 3
    n = SIDE * x_rows.shape[-1]
    left_i = to_col(slab(x_rows, row))
    left_k = to_col(slab(x_cols, row)) + start_of(n, x_rows.shape[-1], 0)

    def needed(rows, cols, out_rows, out_cols):
        most = rows.shape[-1]
        outs = out_rows.shape[-1]
        keys = flat(rows, True) + start_of(SIDE * most, most, 1)
        others = flat(cols, True)
        out_i = out_rows[row].astype(jnp.float32)
        out_j = nt(eye(outs), out_cols[row])
        result = jnp.zeros((n, SIDE), jnp.float32)
        for c in range(SIDE):
            same_k = left_k == keys[c : c + 1]
            same_j = out_j[:, c : c + 1] == others[c : c + 1]
            hit = (nt(same_k, same_j) > 0.5) & (left_i == out_i[c : c + 1])
            some = jnp.max(hit.astype(jnp.float32), axis=1, keepdims=True)
            result = jnp.where(iota((n, SIDE), 1) == c, some, result)
        return result

    for_y = needed(x_rows, x_cols, y_rows, y_cols)
    for_z = needed(y_rows, y_cols, z_rows, z_cols) * (1.0 - for_y)
    group = iota((n, n), 0) >> 3 & 3
    same = group == (iota((n, n), 1) >> 3 & 3)
    before = same & (iota((n, n), 1) <= iota((n, n), 0))
    total_y, total_z = nn(same, for_y), nn(same, for_z)
    ranks = jnp.where(
        for_y > 0.5, nn(before, for_y), jnp.where(for_z > 0.5, total_y + nn(before, for_z), 0.0)
    )
    crosses = (iota((n, SIDE), 0) >> 3 & 3) != (iota((n, SIDE), 1) & 3)
    over = crosses & ((total_y > LEFT_FIRST) | (total_y + total_z > LEFT_ALL))
    flag = jnp.max(over.astype(jnp.float32))

    lane = iota((1, n), 1)
    place = (ring_piece((lane >> 5) - x & 3) * 8 + (lane & 7)).astype(jnp.float32)
    mine = (iota((n, 1), 0) >> 3 & 3) == b
    rows = [message(ranks, (x << 2) + (b ^ d), mine, place) for d in (1, 2, 3)]
    send[...] = table_of(rows, flag)
    rank = nt(iota((8, SIDE), 1) == col, ranks)[:1]
    d = (lane >> 3 & 3) ^ b
    spot = jnp.where(d == 0, place, (d * MOST).astype(jnp.float32) + jnp.maximum(rank - 1.0, 0.0))
    positions[...] = jnp.broadcast_to(spot, (8, n)).astype(jnp.int32)


def terms_list(out_i, out_j, left_i, left_k, left_pos, right_k, right_j, right_pos):
    outs, size = out_i.shape[0], left_i.shape[1]
    found = nt(jnp.where(out_j == right_j, right_pos + 1.0, 0.0), left_k == right_k)
    hit = (out_i == left_i) & (found > 0.5)
    marks = hit.astype(jnp.float32)
    rank = nn(marks, iota((size, size), 0) <= iota((size, size), 1))
    code = left_pos * 256.0 + (found - 1.0)
    lane = iota((outs, 128), 1)
    table = jnp.where(lane == COUNT, jnp.sum(marks, axis=1, keepdims=True), 0.0)
    for q in range(TERMS):
        picked = jnp.where(hit & (rank == q + 1.0), code, 0.0)
        table = table + jnp.where(lane == q, jnp.sum(picked, axis=1, keepdims=True), 0.0)
    multi = (jnp.sum(marks, axis=1, keepdims=True) > 1.5).astype(jnp.float32)
    multi = jnp.broadcast_to(multi, (outs, 128))
    order = nn(iota((outs, outs), 1) <= iota((outs, outs), 0), multi)
    slots = (multi > 0.5) & (order == (lane - (MULTI - 1)).astype(jnp.float32))
    entries = nn(iota((8, outs), 1), slots)[:1]
    entries = entries + jnp.where(lane[:1] == MULTIS, jnp.sum(multi, axis=0, keepdims=True), 0.0)
    table = table + jnp.where(iota((outs, 128), 0) == 0, entries, 0.0)
    return table, lane


def right_kernel(
    at, left_send, positions, x_rows, x_cols, y_rows, y_cols, z_rows, z_cols, send, y_plan, z_plan
):
    row, col = at[0], at[1]
    z, y, k = row >> 3, row >> 1 & 3, row & 1
    most, y_most, z_most = x_rows.shape[-1], y_rows.shape[-1], z_rows.shape[-1]
    n, m = SIDE * most, SIDE * y_most
    rows_i = flat(x_rows, False)
    rows_k = flat(x_cols, False) + start_of(n, most, 1)
    y_i = pick_row(flat(y_rows, True), col)[:1]
    y_j = pick_row(flat(y_cols, True), col)[:1]
    key = to_col(y_i) + start_of(m, y_most, 0)
    other = to_col(y_j)
    tile = iota((SIDE, SIDE * SIDE), 1)
    ours = (tile >> 4 == iota((SIDE, SIDE * SIDE), 0)) & ((tile & 15) == col)
    z_i = nn(ours, z_rows[...].reshape(SIDE * SIDE, z_most))
    z_j = nn(ours, z_cols[...].reshape(SIDE * SIDE, z_most))
    z_t = nt(eye(z_most), z_i)
    need = jnp.zeros((m, SIDE), jnp.float32)
    for r in range(SIDE):
        same_k = key == rows_k[r : r + 1]
        same_i = z_t[:, r : r + 1] == rows_i[r : r + 1]
        hit = (nt(same_k, same_i) > 0.5) & (other == z_j[r : r + 1])
        some = jnp.max(hit.astype(jnp.float32), axis=1, keepdims=True)
        need = jnp.where(iota((m, SIDE), 1) == r, some, need)
    need = nn(need, iota((SIDE, 8), 0) >> 1 == iota((SIDE, 8), 1)) > 0.5
    same = iota((m, m), 0) >> 4 == iota((m, m), 1) >> 4
    before = same & (iota((m, m), 1) <= iota((m, m), 0))
    ranks = jnp.where(need, nn(before, need), 0.0)
    crosses = (iota((m, 8), 0) >> 5 & 3) != (iota((m, 8), 1) & 3)
    over = crosses & (nn(same, need) > RIGHT_FIRST)
    flag = jnp.max(over.astype(jnp.float32))

    lane = iota((1, m), 1)
    slot = (lane & 15).astype(jnp.float32)
    tile = iota((m, 1), 0) >> 4
    dests = [(z << 2) + (y + d & 3) for d in (1, 3, 2)]
    rows = [message(ranks, dest, tile == row, slot) for dest in dests]
    send[:8] = table_of(rows, flag)
    rows = [message(ranks, dest, tile == (row ^ 8), slot) for dest in dests]
    send[8:] = table_of(rows, flag)
    rank = nt(iota((8, 8), 1) == row >> 1, ranks)[:1]
    piece = ring_piece((lane >> 5 & 3) - y & 3)
    spot = jnp.where(piece == 0, slot, jnp.maximum(rank - 1.0, 0.0))
    base = (lane >> 4 & 1 ^ k) * 128 + piece * MOST + (lane >> 7 ^ z) * 16
    y_pos = base.astype(jnp.float32) + spot
    lane = iota((1, n), 1)
    piece = ring_piece((lane >> 4 & 3) - y & 3)
    x_pos = (lane >> 3 & 1 ^ k) * 64 + piece * 16 + (lane >> 6 ^ z) * 8 + (lane & 7)
    x_pos = x_pos.astype(jnp.float32)

    x_k = pick_row(flat(x_rows, True), col)[:1] + start_of(n, most, 1)
    x_j = pick_row(flat(x_cols, True), col)[:1]
    left_i = slab(x_rows, row)
    left_k = to_col(slab(x_cols, row)) + start_of(n, most, 0)
    left_pos = positions[:1].astype(jnp.float32)

    def own(table):
        return pick_row(table[row], col)[:1]

    left_flag = left_send[3, 0].astype(jnp.float32)
    table, lane = terms_list(
        to_col(own(y_rows)), to_col(own(y_cols)), left_i, left_k, left_pos, x_k, x_j, x_pos
    )
    y_plan[...] = jnp.where(lane == FLAG, left_flag, table).astype(jnp.int32)
    out_i, out_j = to_col(own(z_rows)), to_col(own(z_cols))
    table, lane = terms_list(
        out_i, out_j, left_i, left_k, left_pos,
        y_i + start_of(m, y_most, 1), y_j, y_pos,
    )
    here = (own(x_rows) == out_i) & (own(x_cols) == out_j)
    slot = (iota(here.shape, 1) + 1).astype(jnp.float32)
    slot = jnp.sum(jnp.where(here, slot, 0.0), axis=1, keepdims=True)
    table = table + jnp.where(lane == OWN, slot, 0.0)
    table = jnp.where(lane == FLAG, left_flag + 2.0 * flag, table)
    z_plan[...] = table.astype(jnp.int32)


def pack_kernel(unit, count, parts, given, *refs):
    sources, outs = refs[:count], refs[count : count + len(parts)]
    held, table, in_sems, out_sems = refs[count + len(parts) :]
    loads = [pltpu.make_async_copy(given, table, in_sems.at[count])]
    loads += [
        pltpu.make_async_copy(source, held.at[pl.ds(n * unit, unit)], in_sems.at[n])
        for n, source in enumerate(sources)
    ]
    for load in loads:
        load.start()
    for load in loads:
        load.wait()
    copies = []
    for (row, first, last), out in zip(parts, outs):
        for n in range(last - first):
            copies.append(
                pltpu.make_async_copy(
                    held.at[table[row, first + n]], out.at[n], out_sems.at[len(copies)]
                )
            )
    for copy in copies:
        copy.start()
    for copy in copies:
        copy.wait()


def pack(table, sources, *parts):
    unit = sources[0].shape[0]
    sizes = [last - first for _, first, last in parts]
    return pl.pallas_call(
        functools.partial(pack_kernel, unit, len(sources), parts),
        out_shape=[jax.ShapeDtypeStruct((size, BLOCK, BLOCK), jnp.bfloat16) for size in sizes],
        in_specs=[pl.BlockSpec(memory_space=pl.ANY)] * (1 + len(sources)),
        out_specs=[pl.BlockSpec(memory_space=pl.ANY)] * len(sizes),
        scratch_shapes=[
            pltpu.VMEM((unit * len(sources), BLOCK, BLOCK), jnp.bfloat16),
            pltpu.SMEM(table.shape, jnp.int32),
            pltpu.SemaphoreType.DMA((len(sources) + 1,)),
            pltpu.SemaphoreType.DMA((sum(sizes),)),
        ],
    )(table, *sources)


def nothing(sizes):
    return pl.pallas_call(
        lambda *refs: None,
        out_shape=[jax.ShapeDtypeStruct((size, BLOCK, BLOCK), jnp.bfloat16) for size in sizes],
        out_specs=[pl.BlockSpec(memory_space=pl.ANY)] * len(sizes),
    )()


def products_kernel(layout, update, given, *refs):
    pieces = refs[: len(layout)]
    out, left, right, plan, sems = refs[len(layout) :]
    fetch = pltpu.make_async_copy(given, plan, sems.at[len(layout)])
    fetch.start()

    def copy(n):
        side, at, skip, size, _ = layout[n]
        buffer = (left, right)[side]
        source = pieces[n] if skip is None else pieces[n].at[pl.ds(skip, size)]
        sem = sems.at[n if layout[n][4] else len(layout) + 1 + side]
        return pltpu.make_async_copy(source, buffer.at[pl.ds(at, size)], sem)

    def each(act, flagged):
        for n, piece in enumerate(layout):
            if (piece[4] > 0) != flagged:
                continue
            if flagged:

                @pl.when(flag & piece[4] != 0)
                def _():
                    act(copy(n))

            else:
                act(copy(n))

    each(lambda c: c.start(), False)
    fetch.wait()
    flag = plan[0, FLAG]

    @pl.when(flag > 0)
    def _():
        each(lambda c: c.start(), True)
        each(lambda c: c.wait(), True)

    for side, buffer in enumerate((left, right)):
        total = sum(piece[3] for piece in layout if piece[0] == side and not piece[4])
        span = buffer.at[pl.ds(0, total)]
        pltpu.make_async_copy(span, span, sems.at[len(layout) + 1 + side]).wait()

    def product(t, q):
        code = plan[t, q]
        return jnp.dot(
            left[code >> 8], right[code & 255], preferred_element_type=jnp.float32
        )

    def write(t, value):
        if update:
            slot = plan[t, OWN]
            x_here = left[jnp.maximum(slot - 1, 0)].astype(jnp.float32)
            value = 1.5 * jnp.where(slot > 0, x_here, 0.0) - 0.5 * value
        out[t] = value.astype(jnp.bfloat16)

    for t in range(out.shape[0]):
        write(t, jnp.where(plan[t, COUNT] > 0, product(t, 0), 0.0))

    def again(n, carry):
        t = plan[0, MULTI + n]
        terms = plan[t, COUNT]
        write(t, lax.fori_loop(1, terms, lambda q, total: total + product(t, q), product(t, 0)))
        return carry

    lax.fori_loop(0, plan[0, MULTIS], again, 0)


def products(plan, pieces, sizes, update):
    outs = plan.shape[0]
    layout = [
        (side, at, skip, p.shape[0] - (skip or 0), bit) for side, at, skip, bit, p in pieces
    ]
    return pl.pallas_call(
        functools.partial(products_kernel, layout, update),
        out_shape=jax.ShapeDtypeStruct((outs, BLOCK, BLOCK), jnp.bfloat16),
        in_specs=[pl.BlockSpec(memory_space=pl.ANY)] * (1 + len(pieces)),
        out_specs=pl.BlockSpec(memory_space=pltpu.VMEM),
        scratch_shapes=[
            pltpu.VMEM((sizes[0], BLOCK, BLOCK), jnp.bfloat16),
            pltpu.VMEM((sizes[1], BLOCK, BLOCK), jnp.bfloat16),
            pltpu.SMEM(plan.shape, jnp.int32),
            pltpu.SemaphoreType.DMA((len(pieces) + 3,)),
        ],
        compiler_params=pltpu.CompilerParams(vmem_limit_bytes=32 * 1024 * 1024),
    )(plan, *[p[-1] for p in pieces])


def row_send(blocks, perm):
    return lax.ppermute(blocks, "row", perm)


def col_send(blocks, perm):
    return lax.ppermute(blocks, "col", perm)


def after(value, *others):
    return lax.optimization_barrier((value, others))[0]


def shards(x_blocks, x_rows, x_cols, y_rows, y_cols, z_rows, z_cols):
    row = lax.axis_index("row")
    col = lax.axis_index("col")
    at = jnp.stack([row, col]).astype(jnp.int32)
    tables = (x_rows, x_cols, y_rows, y_cols, z_rows, z_cols)
    tile = x_blocks[0, 0]
    y_most, z_most = y_rows.shape[-1], z_rows.shape[-1]
    smem = pl.BlockSpec(memory_space=pltpu.SMEM)
    vmem = pl.BlockSpec(memory_space=pltpu.VMEM)

    far = row_send(tile, Z_SWAP)
    near = [col_send(tile, ring) for ring in X_RING]
    left_send, positions = pl.pallas_call(
        left_kernel,
        out_shape=(jax.ShapeDtypeStruct((8, 128), jnp.int32),) * 2,
        in_specs=[smem] + [vmem] * 6,
    )(at, *tables)
    near, left_send, positions = lax.optimization_barrier((near, left_send, positions))
    quad = [tile] + near
    ends = (LEFT_FIRST, LEFT_ALL, LEFT_FIRST)
    parts = [(d, 0, end) for d, end in enumerate(ends)]
    parts += [(d, LEFT_FIRST, LEFT_ALL) for d in (0, 2)]
    first = pack(left_send, quad, *parts)
    first, second = first[:3], first[3:]
    one, two = [col_send(blocks, swap) for blocks, swap in zip(first[:2], B_SWAP[:2])]
    first = [one, two, col_send(after(first[2], one), B_SWAP[2])]
    pair = jnp.concatenate([tile, far])
    across, up, down = [row_send(pair, Y_RING[n]) for n in (2, 0, 1)]
    right_send, y_plan, z_plan = pl.pallas_call(
        right_kernel,
        out_shape=(
            jax.ShapeDtypeStruct((16, 128), jnp.int32),
            jax.ShapeDtypeStruct((y_most, 128), jnp.int32),
            jax.ShapeDtypeStruct((z_most, 128), jnp.int32),
        ),
        in_specs=[smem, smem] + [vmem] * 7,
    )(at, left_send, positions, *tables)
    first, up, down, across, right_send, y_plan, z_plan = lax.optimization_barrier(
        (first, up, down, across, right_send, y_plan, z_plan)
    )
    x_half = [pair, up, down, across]
    x_mate = [row_send(blocks, CORE_SWAP) for blocks in x_half]

    def more_left():
        rest = pack(left_send, quad, *[(d, end, MOST) for d, end in enumerate(ends)])
        return tuple(col_send(blocks, swap) for blocks, swap in zip(rest, B_SWAP))

    rest = lax.cond(
        left_send[3, 0] > 0, more_left, lambda: tuple(nothing([MOST - end for end in ends]))
    )

    left = [(0, 8 * n, None, 0, p) for n, p in enumerate(quad)]
    left += [(0, MOST * (n + 1), None, 0, p) for n, p in enumerate(first)]
    right = [(1, 16 * n, None, 0, p) for n, p in enumerate(x_half + x_mate)]
    extra = [(0, MOST * (n + 1) + end, None, 1, p) for n, (end, p) in enumerate(zip(ends, rest))]
    y_tile = products(y_plan, left + right + extra, (4 * MOST, 128), False)

    y_far = row_send(y_tile, Z_SWAP)
    tile_mate = row_send(y_tile, CORE_SWAP)
    own_send = pack(right_send, [y_tile], *[(d, 0, RIGHT_FIRST) for d in range(3)])
    own_near = [row_send(blocks, ring) for blocks, ring in zip(own_send, Y_RING)]
    y_far, tile_mate, own_near = lax.optimization_barrier((y_far, tile_mate, own_near))
    own_mate = [row_send(blocks, CORE_SWAP) for blocks in own_near]
    far_send = pack(right_send, [y_far], *[(8 + d, 0, RIGHT_FIRST) for d in range(3)])
    far_mate = row_send(y_far, CORE_SWAP)
    far_send, far_mate, own_mate, second = lax.optimization_barrier(
        (far_send, far_mate, own_mate, second)
    )
    far_near = [row_send(blocks, ring) for blocks, ring in zip(far_send, Y_RING)]
    second = [col_send(blocks, swap) for blocks, swap in zip(second, B_SWAP[::2])]
    far_near, second = lax.optimization_barrier((far_near, second))
    far_near_mate = [row_send(blocks, CORE_SWAP) for blocks in far_near]

    def more_right():
        blocks = pack(right_send, [y_tile], *[(d, RIGHT_FIRST, y_most) for d in range(3)])
        blocks += pack(right_send, [y_far], *[(8 + d, RIGHT_FIRST, y_most) for d in range(3)])
        blocks = [row_send(b, ring) for b, ring in zip(blocks, Y_RING + Y_RING)]
        return tuple(blocks + [row_send(b, CORE_SWAP) for b in blocks])

    more = lax.cond(
        right_send[3, 0] > 0, more_right, lambda: tuple(nothing([y_most - RIGHT_FIRST] * 12))
    )

    left += [(0, MOST * (2 * n + 1) + LEFT_FIRST, None, 0, p) for n, p in enumerate(second)]
    extra = [
        (0, MOST * (n + 1) + LEFT_ALL, LEFT_ALL - end, 1, p)
        for n, (end, p) in enumerate(zip(ends, rest))
    ]
    right = []
    spots = [i * MOST + j * y_most for i in range(4) for j in range(2)]
    ours = [y_tile, y_far] + [p for both in zip(own_near, far_near) for p in both]
    theirs = [tile_mate, far_mate] + [p for both in zip(own_mate, far_near_mate) for p in both]
    for n, side in enumerate((ours, theirs)):
        right += [(1, n * 128 + spot, None, 0, p) for spot, p in zip(spots, side)]
        rest_spots = spots[2::2] + spots[3::2]
        extra += [
            (1, n * 128 + spot + RIGHT_FIRST, None, 2, p)
            for spot, p in zip(rest_spots, more[6 * n : 6 * n + 6])
        ]
    update = products(z_plan, left + right + extra, (4 * MOST, 8 * MOST), True)
    return (y_tile[None, None], update[None, None])


def solution(mesh):
    in_specs = (P("row", "col", None, None, None), P(), P(), P(), P(), P(), P())
    out_specs = (P("row", "col", None, None, None), P("row", "col", None, None, None))
    return jax.shard_map(shards, mesh=mesh, in_specs=in_specs, out_specs=out_specs, check_vma=False)
```
